128 devices in a mesh: row: 8 (over x, core), col: 16 (over y, z).
Axes of the slice: x: 4, y: 4, z: 4, core: 2. Of those that a mesh axis runs over, the one named last changes fastest.
Arguments:
- amplitudes: float32 [8, 4, 8, 16, 128, 128], P(None, None, None, 'col', 'row'), may hold values from -6 to 6
- coupling: float32 [8, 6, 128, 8, 16, 128], P(None, None, 'col', None, 'row'), may hold values from -0.0625 to 0.0625
- incoming_residual: float32 [8, 4, 8, 6, 128, 128], P('row', None, None, None, 'col'), may hold values from -6 to 6
- occupied_count: int32 [8], replicated, may hold values from 8 to 16, as said below
- virtual_count: int32 [8], replicated, may hold values from 64 to 128, as said below
Outputs:
- residual_out: float32 [8, 4, 8, 6, 128, 128], P('row', None, None, None, 'col')
The draws below stay inside these ranges and needn't reach their ends.
Inputs may be any that keep to these rules, and one draw needn't show every extreme that they name: `occupied_count`: some irrep has exactly 16 and some exactly 8 occupied orbitals. `virtual_count`: some irrep has exactly 128 and some exactly 64 virtual orbitals.
All inputs are finite; a program needn't handle non-finite values.
Results may differ from the reference program's by a relative error of at most 0.00005.
Values sent between devices are 32-bit elements; how exact they have to be, the bound alone decides.
No kernel may reach another device: no remote copies, remote signals or barrier semaphores. Data moves between devices by JAX's collectives and lax.ppermute only.
A program may use at most 256 MiB of HBM per device.

```python
import jax
import jax.numpy as jnp
from jax import lax

SYMMETRY_SPECIES = 8
OCCUPIED_PADDED = 16
VIRTUAL_PADDED = 128
OCCUPIED_I_COUNT = 4
OCCUPIED_J_COUNT = 6


def sampled_count(key, low, high):
    values = jax.random.randint(key, (SYMMETRY_SPECIES,), low, high + 1).astype(jnp.int32)
    order = jax.random.permutation(jax.random.fold_in(key, 17), SYMMETRY_SPECIES)
    values = values.at[order[0]].set(high)
    values = values.at[order[1]].set(low)
    return values.astype(jnp.int32)


def draw_occupied_count(key, part):
    key = jax.random.fold_in(key, 3)
    return sampled_count(key, OCCUPIED_PADDED // 2, OCCUPIED_PADDED)


def draw_virtual_count(key, part):
    key = jax.random.fold_in(key, 5)
    return sampled_count(key, VIRTUAL_PADDED // 2, VIRTUAL_PADDED)


def level_of(rng, extent, split, low, largest):
    loudness = 1.0
    for axis_at, parts in split:
        draws = jax.random.uniform(jax.random.fold_in(jax.random.fold_in(rng, 6), axis_at), (parts,), jnp.float32, low / len(split), largest / len(split))
        loudness = loudness * jnp.repeat(jnp.exp(draws), extent[axis_at] // parts).reshape((-1,) + (1,) * (len(extent) - 1 - axis_at))
    return loudness


def scatter_about(key, extent, width, limit, pieces=(), held_as=jnp.bfloat16):
    result = width * jax.random.normal(key, extent, jnp.float32)
    if pieces:
        result = result * level_of(key, extent, pieces, -0.22, 0.18)
    return jnp.clip(result, -limit, limit).astype(held_as)


def setup_inputs(seed: int = 0) -> dict:
    keys = jax.random.split(jax.random.key(seed), 6)
    return {
        "amplitudes": scatter_about(keys[0], (SYMMETRY_SPECIES, OCCUPIED_I_COUNT, SYMMETRY_SPECIES, OCCUPIED_PADDED, VIRTUAL_PADDED, VIRTUAL_PADDED), 1.0, 6.0, ((3, 16), (4, 8)), jnp.float32),
        "coupling": scatter_about(keys[1], (SYMMETRY_SPECIES, OCCUPIED_J_COUNT, VIRTUAL_PADDED, SYMMETRY_SPECIES, OCCUPIED_PADDED, VIRTUAL_PADDED), (SYMMETRY_SPECIES * OCCUPIED_PADDED * VIRTUAL_PADDED // 2) ** -0.5, 0.0625, ((2, 16), (4, 8)), jnp.float32),
        "incoming_residual": scatter_about(keys[2], (SYMMETRY_SPECIES, OCCUPIED_I_COUNT, SYMMETRY_SPECIES, OCCUPIED_J_COUNT, VIRTUAL_PADDED, VIRTUAL_PADDED), 1.0, 6.0, ((0, 8), (4, 16)), jnp.float32),
        "occupied_count": draw_occupied_count(jax.random.fold_in(keys[5], 71), 0),
        "virtual_count": draw_virtual_count(jax.random.fold_in(keys[5], 71), 0),
    }


def reference(amplitudes, coupling, incoming_residual, occupied_count, virtual_count):
    occ_index = jnp.arange(OCCUPIED_PADDED, dtype=jnp.int32)
    virtual_index = jnp.arange(VIRTUAL_PADDED, dtype=jnp.int32)
    keep_occupied = (occ_index[None, :] < occupied_count[:, None]).astype(jnp.float32)
    keep_virtual = (virtual_index[None, :] < virtual_count[:, None]).astype(jnp.float32)
    masked_amps = amplitudes * keep_virtual[:, None, None, None, None, :] * keep_occupied[None, None, :, :, None, None] * keep_virtual[None, None, :, None, :, None]
    masked_coupling = coupling * keep_virtual[:, None, :, None, None, None] * keep_occupied[None, None, None, :, :, None] * keep_virtual[None, None, None, :, None, :]
    cycle_term = jnp.einsum("xiykca,gjbykc->xigjba", masked_amps, masked_coupling, precision=lax.Precision.HIGHEST, preferred_element_type=jnp.float32)
    return incoming_residual + cycle_term
```

```python
import functools

import jax
import jax.numpy as jnp
from jax import lax
from jax.experimental import pallas as pl
from jax.experimental.pallas import tpu as pltpu
from jax.sharding import Mesh
from jax.sharding import PartitionSpec as P

NX, NC, NY, NZ = 4, 2, 4, 4
F32 = jnp.float32
BF16 = jnp.bfloat16


def split(x):
    hi = x.astype(BF16)
    lo = (x - hi.astype(F32)).astype(BF16)
    return hi, lo


ROWS_B = 96


def pack_b_kernel(info, b_ref, o_ref, acc, *, width):
    e = jnp.bitwise_xor(info[0], pl.program_id(1))
    acc[...] = jnp.zeros_like(acc)
    row = lax.broadcasted_iota(jnp.int32, (128, 256), 0)
    col = lax.broadcasted_iota(jnp.int32, (128, 256), 1)
    for y in range(8):
        off = info[1 + y]
        count = info[9 + y]
        tile = off // 128
        x = b_ref[pl.ds(2 * y + e, ROWS_B, stride=16), :]
        hi, lo = split(x)
        place = ((col == row + (off - tile * 128)) & (row < count)).astype(F32).astype(BF16)
        moved = jnp.dot(hi, place, preferred_element_type=F32)
        moved += jnp.dot(lo, place, preferred_element_type=F32)
        at = pl.ds(pl.multiple_of(tile * 128, 128), 256)
        acc[:, at] = acc[:, at] + moved
    o_ref[0] = acc[:, :width]


def pack_b(info, b2, width):
    rows = b2.shape[0] // 16
    return pl.pallas_call(
        functools.partial(pack_b_kernel, width=width),
        grid_spec=pltpu.PrefetchScalarGridSpec(
            num_scalar_prefetch=1,
            grid=(rows // ROWS_B, 2),
            in_specs=[pl.BlockSpec((ROWS_B * 16, 128), lambda r, u, info: (r, 0))],
            out_specs=pl.BlockSpec((1, ROWS_B, width), lambda r, u, info: (u, r, 0)),
            scratch_shapes=[pltpu.VMEM((ROWS_B, width + 256), F32)],
        ),
        out_shape=jax.ShapeDtypeStruct((2, rows, width), F32),
        compiler_params=pltpu.CompilerParams(vmem_limit_bytes=32 * 2**20),
        cost_estimate=pl.CostEstimate(
            flops=2 * 2 * 2 * rows * 1024 * 256, bytes_accessed=4 * rows * (2048 + 2 * width), transcendentals=0
        ),
        name="pack_coupling",
    )(info, b2)


def pack_a_kernel(tgt_ref, a0, a1, a2, a3, o_ref, hi_s, lo_s):
    step = pl.program_id(0)

    @pl.when(step == 0)
    def _():
        for s, ref in enumerate((a0, a1, a2, a3)):
            for cr in range(2):
                for i in range(4):
                    hi, lo = split(ref[cr, i])
                    at = (s * 2 + cr) * 128
                    hi_s[at : at + 128, i * 128 : (i + 1) * 128] = hi
                    lo_s[at : at + 128, i * 128 : (i + 1) * 128] = lo

    rows = lax.broadcasted_iota(jnp.int32, (128, 1024), 0) + step * 128
    pick = (rows == tgt_ref[...]).astype(F32).astype(BF16)
    out = jnp.dot(pick, hi_s[...], preferred_element_type=F32)
    out += jnp.dot(pick, lo_s[...], preferred_element_type=F32)
    o_ref[...] = out


def pack_a(tgt, parts, width):
    full = pl.BlockSpec((2, 4, 128, 128), lambda p: (0, 0, 0, 0))
    return pl.pallas_call(
        pack_a_kernel,
        grid=(width // 128,),
        in_specs=[pl.BlockSpec((1, 1024), lambda p: (0, 0))] + [full] * 4,
        out_specs=pl.BlockSpec((128, 512), lambda p: (p, 0)),
        scratch_shapes=[pltpu.VMEM((1024, 512), BF16), pltpu.VMEM((1024, 512), BF16)],
        out_shape=jax.ShapeDtypeStruct((width, 512), F32),
        compiler_params=pltpu.CompilerParams(vmem_limit_bytes=32 * 2**20),
        cost_estimate=pl.CostEstimate(
            flops=2 * 2 * width * 1024 * 512, bytes_accessed=4 * (2**19 + width * 512), transcendentals=0
        ),
        name="pack_amplitudes",
    )(tgt, *parts)


def shift_x(value, by):
    return lax.ppermute(value, "x", [(p, (p + by) % NX) for p in range(NX)])


def swap_core(value):
    return lax.ppermute(value, "c", [(0, 1), (1, 0)])


def to_k_owner(value, u):
    pairs = []
    for c in range(NC):
        for z in range(NZ):
            pairs.append((c * NZ + z, (z // 2) * NZ + 2 * c + ((z % 2) ^ u)))
    return lax.ppermute(value, ("c", "z"), pairs)


def to_home(value, u, w):
    pairs = []
    for c in range(NC):
        for z in range(NZ):
            pairs.append((c * NZ + z, ((z // 2) ^ w) * NZ + 2 * c + ((z % 2) ^ u)))
    return lax.ppermute(value, ("c", "z"), pairs)


def dot3(b, a):
    return lax.dot_general(
        b, a, (((1,), (0,)), ((), ())), precision=lax.Precision.HIGH, preferred_element_type=F32
    )


def body(amplitudes, coupling, incoming_residual, occupied_count, virtual_count, *, width):
    xi, ci, yi, zi = (lax.axis_index(n) for n in ("x", "c", "y", "z"))
    offsets = jnp.cumsum(virtual_count) - virtual_count
    info = jnp.concatenate([jnp.stack([zi % 2]), offsets, virtual_count]).astype(jnp.int32)

    amps = amplitudes.reshape(4, 2, 4, 128, 128)
    own = lax.dynamic_index_in_dim(amps, ci, 1, keepdims=False)
    got = swap_core(lax.dynamic_index_in_dim(amps, 1 - ci, 1, keepdims=False))
    both = jnp.stack([own, got])
    parts = []
    for s in range(4):
        msg = lax.dynamic_index_in_dim(both, (xi + s) % 4, 1, keepdims=False)
        parts.append(msg if s == 0 else shift_x(msg, s))

    k = yi * 4 + zi
    src_x = (xi - jnp.arange(4, dtype=jnp.int32)) % 4
    src_c = jnp.stack([ci, 1 - ci])
    chunk = 2 * src_x[:, None] + src_c[None, :]
    c_at = 16 * chunk[:, :, None, None] + jnp.arange(16, dtype=jnp.int32)
    keep = (c_at < virtual_count[:, None]) & (k < occupied_count)[:, None]
    tgt = jnp.where(keep, offsets[:, None] + c_at, -1).reshape(1, 1024).astype(jnp.int32)

    packed_b = pack_b(info, coupling.reshape(-1, 128), width)
    blocks = [to_k_owner(packed_b[u], u) for u in range(2)]

    packed_a = pack_a(tgt, parts, width)
    a_own = lax.all_gather(packed_a, "y", axis=0, tiled=False)
    a_oth = swap_core(a_own)

    def terms(b, source):
        return [dot3(b, lax.dynamic_index_in_dim(a, source, 0, keepdims=False)) for a in (a_own, a_oth)]

    h = zi // 2
    total = []
    for u in range(2):
        b = blocks[u]
        half = b.shape[0] // 2
        left, right = shift_x(b, 1), shift_x(b, -1)
        far_top, far_low = shift_x(left[:half], 1), shift_x(right[half:], -1)
        far = jnp.concatenate([far_top, far_low])
        sums = None
        for piece, dx in ((b, 0), (left, -1), (right, 1), (far, 2)):
            new = terms(piece, (xi + dx) % 4)
            sums = new if sums is None else [p + q for p, q in zip(sums, new)]
        for w in range(2):
            pick_own = ci == jnp.bitwise_xor(h, w)
            total.append(to_home(jnp.where(pick_own, sums[0], sums[1]), u, w))

    cycle = (total[0] + total[1]) + (total[2] + total[3])
    x_at = 2 * xi + ci
    b_at = 8 * (4 * yi + zi) + jnp.arange(8, dtype=jnp.int32)
    keep_b = (b_at[None, :] < virtual_count[:, None])[None, :, None, :, None]
    keep_a = jnp.arange(128, dtype=jnp.int32) < virtual_count[x_at]
    cycle = cycle.reshape(8, 6, 8, 4, 128).transpose(3, 0, 1, 2, 4)
    cycle = jnp.where(keep_b & keep_a, cycle, 0.0)
    return incoming_residual + cycle[None]


def solution(mesh):
    fine = Mesh(mesh.devices.reshape(NX, NC, NY, NZ), ("x", "c", "y", "z"))
    return jax.shard_map(
        functools.partial(body, width=1024),
        mesh=fine,
        in_specs=(
            P(None, None, None, ("y", "z"), ("x", "c"), None),
            P(None, None, ("y", "z"), None, ("x", "c"), None),
            P(("x", "c"), None, None, None, ("y", "z"), None),
            P(),
            P(),
        ),
        out_specs=P(("x", "c"), None, None, None, ("y", "z"), None),
        check_vma=False,
    )
```

```python
import functools

import jax
import jax.numpy as jnp
from jax import lax
from jax.experimental import pallas as pl
from jax.experimental.pallas import tpu as pltpu
from jax.sharding import Mesh
from jax.sharding import PartitionSpec as P

NX, NC, NY, NZ = 4, 2, 4, 4
F32 = jnp.float32
BF16 = jnp.bfloat16
VMEM = 60 * 2**20
ORDER = (0, 1)
WIDTHS = (768, 896, 1024)
COST = pl.CostEstimate(flops=1, bytes_accessed=1, transcendentals=0)
LONG = pl.CostEstimate(flops=2 * 10**10, bytes_accessed=7 * 10**7, transcendentals=0)


def split(x):
    hi = x.astype(BF16)
    lo = (x - hi.astype(F32)).astype(BF16)
    return hi, lo


VIR, OCC, X, C, Y, Z = 0, 8, 16, 17, 18, 19


def scalars(occupied_count, virtual_count):
    place = jnp.stack([lax.axis_index(n) for n in ("x", "c", "y", "z")])
    return jnp.concatenate([virtual_count, occupied_count, place]).astype(jnp.int32)


def params(**more):
    return dict(compiler_params=pltpu.CompilerParams(vmem_limit_bytes=VMEM), cost_estimate=COST, **more)


ROWS_B = 96


def pack_b_kernel(info, b_ref, after, *refs):
    outs, acc = refs[:2], refs[2]
    width = outs[0].shape[1]
    lane = lax.broadcasted_iota(jnp.int32, (ROWS_B, 128), 1)
    for u, o_ref in zip(ORDER, outs):
        e = jnp.bitwise_xor(jnp.bitwise_and(info[Z], 1), u)
        acc[...] = jnp.zeros_like(acc)
        off = 0
        for y in range(8):
            count = info[VIR + y]
            tile = off // 128
            start = off - tile * 128
            x = pltpu.roll(b_ref[pl.ds(2 * y + e, ROWS_B, stride=16), :], start, 1)
            here = pl.ds(pl.multiple_of(tile * 128, 128), 128)
            there = pl.ds(pl.multiple_of(tile * 128 + 128, 128), 128)
            acc[:, here] += jnp.where((lane >= start) & (lane < start + count), x, 0.0)
            acc[:, there] += jnp.where(lane < start + count - 128, x, 0.0)
            off += count
        o_ref[...] = acc[:, :width]


def pack_b(info, b2, after, width):
    rows = b2.shape[0] // 16
    out = pl.BlockSpec((ROWS_B, width), lambda r, info: (r, 0))
    return pl.pallas_call(
        pack_b_kernel,
        grid_spec=pltpu.PrefetchScalarGridSpec(
            num_scalar_prefetch=1,
            grid=(rows // ROWS_B,),
            in_specs=[
                pl.BlockSpec((ROWS_B * 16, 128), lambda r, info: (r, 0)),
                pl.BlockSpec(memory_space=pl.ANY),
            ],
            out_specs=[out, out],
            scratch_shapes=[pltpu.VMEM((ROWS_B, width + 256), F32)],
        ),
        out_shape=[jax.ShapeDtypeStruct((rows, width), F32)] * 2,
        **params(name="pack_coupling"),
    )(info, b2, after)


def pack_a_kernel(info, own, left, right, far0, far1, sib, after, o_ref, acc):
    acc[...] = jnp.zeros_like(acc)
    row = lax.broadcasted_iota(jnp.int32, (24, 128), 0)
    k = 4 * info[Y] + info[Z]
    core = info[C]
    for s in range(4):
        for cr in range(2):
            first = 32 * jnp.bitwise_and(info[X] + 4 - s, 3) + 16 * jnp.bitwise_xor(core, cr)
            off = first
            for y in range(8):
                valid = jnp.where(k < info[OCC + y], info[VIR + y] - first, 0)
                base = off // 8 * 8
                start = off - base

                @pl.when(valid > 0)
                def _(s=s, cr=cr, y=y, valid=valid, base=base, start=start):
                    at = pl.ds(pl.multiple_of(base, 8), 24)
                    mine = (row >= start) & (row < start + jnp.minimum(valid, 16))
                    here = slice(16 * y, 16 * (y + 1))
                    for i in range(4):
                        cols = slice(i * 128, (i + 1) * 128)
                        if cr == 1:
                            x = sib[s, i, here, :]
                        elif s == 2:
                            x = jnp.where(core == 0, far0[0, i, here, :], far1[0, i, here, :])
                        else:
                            x = (own, left, None, right)[s][core, i, here, :]
                        x = jnp.pad(x, ((0, 8), (0, 0)))
                        acc[at, cols] = jnp.where(mine, pltpu.roll(x, start, 0), acc[at, cols])

                off += info[VIR + y]

    o_ref[...] = acc[: o_ref.shape[0], :]


def pack_a(info, parts, after, width):
    full = [pl.BlockSpec(p.shape, lambda p, info: (0, 0, 0, 0)) for p in parts]
    return pl.pallas_call(
        pack_a_kernel,
        grid_spec=pltpu.PrefetchScalarGridSpec(
            num_scalar_prefetch=1,
            grid=(1,),
            in_specs=full + [pl.BlockSpec(memory_space=pl.ANY)],
            out_specs=pl.BlockSpec((width, 512), lambda p, info: (0, 0)),
            scratch_shapes=[pltpu.VMEM((width + 24, 512), F32)],
        ),
        out_shape=jax.ShapeDtypeStruct((width, 512), F32),
        **params(name="pack_amplitudes"),
    )(info, *parts, after)


def shift_y(value, by):
    return lax.ppermute(value, "y", [(p, (p + by) % NY) for p in range(NY)])


def shift_x(value, by):
    return lax.ppermute(value, "x", [(p, (p + by) % NX) for p in range(NX)])


def swap_core(value):
    return lax.ppermute(value, "c", [(0, 1), (1, 0)])


def to_k_owner(value, u):
    pairs = []
    for c in range(NC):
        for z in range(NZ):
            pairs.append((c * NZ + z, (z // 2) * NZ + 2 * c + ((z % 2) ^ u)))
    return lax.ppermute(value, ("c", "z"), pairs)


def to_home(value, u, w):
    pairs = []
    for c in range(NC):
        for z in range(NZ):
            pairs.append((c * NZ + z, ((z // 2) ^ w) * NZ + 2 * c + ((z % 2) ^ u)))
    return lax.ppermute(value, ("c", "z"), pairs)


def products_kernel(info, *refs, plan, first, ws, flat):
    count = sum(len(g[1]) for g in plan)
    pieces, a_refs, refs = refs[:count], (refs[count : count + 4], refs[count + 4 : count + 8]), refs[count + 8 :]
    if not first:
        before, refs = refs[0], refs[1:]
    outs, (b_f32, b_both, a_buf, b_sem, a_sem) = refs[:-5], refs[-5:]
    steps = len(plan)
    n = pl.program_id(0)
    w = n // steps
    t = n - w * steps
    rows_all = b_f32.shape[1]

    def fetch_a(n, slot):
        w = n // steps
        t = n - w * steps
        dx = plan[0][0]
        for at, (other, _) in enumerate(plan[1:]):
            dx = jnp.where(t == at + 1, other, dx)
        d = jnp.bitwise_and(info[X] + dx + 4 - info[Y], 3)
        sibling = jnp.bitwise_xor(jnp.bitwise_xor(info[Z] // 2, w + ws[0]), info[C])
        for m, blocks in enumerate(a_refs):
            for way, ref in zip((0, 3, 1, 2), blocks):

                @pl.when((sibling == m) & (d == way))
                def _(ref=ref):
                    pltpu.make_async_copy(ref, a_buf.at[slot], a_sem.at[slot]).start()

    def b_copies(t):
        at = sum(len(g[1]) for g in plan[:t])
        return [
            pltpu.make_async_copy(pieces[at + p].at[pl.ds(start, rows)], b_f32.at[t, pl.ds(row, rows)], b_sem.at[at + p])
            for p, (row, start, rows) in enumerate(plan[t][1])
        ]

    @pl.when(n == 0)
    def _():
        for copy in b_copies(0):
            copy.start()
        fetch_a(0, 0)
        for t in range(1, steps):
            for copy in b_copies(t):
                copy.start()

    @pl.when(n + 1 < len(ws) * steps)
    def _():
        fetch_a(n + 1, (n + 1) % 2)

    for at in range(steps):

        @pl.when(n == at)
        def _(at=at):
            for copy in b_copies(at):
                copy.wait()
            hi, lo = split(b_f32[at])
            b_both[at, :rows_all, :] = hi
            b_both[at, rows_all:, :] = lo

    slot = n % 2
    pltpu.make_async_copy(a_refs[0][0], a_buf.at[slot], a_sem.at[slot]).wait()
    a_hi, a_lo = split(a_buf[slot])
    new2 = jnp.dot(b_both[t], a_hi, preferred_element_type=F32)
    new = new2[:rows_all] + new2[rows_all:]
    new += jnp.dot(b_both[t, :rows_all, :], a_lo, preferred_element_type=F32)

    def add(o_ref):
        @pl.when(t == 0)
        def _():
            if first:
                o_ref[...] = new.reshape(o_ref.shape)
            else:
                o_ref[...] = before[...].reshape(o_ref.shape) + new.reshape(o_ref.shape)

        @pl.when(t > 0)
        def _():
            o_ref[...] += new.reshape(o_ref.shape)

    if flat:
        for at, o_ref in enumerate(outs):
            pl.when(w == at)(functools.partial(add, o_ref))
    else:
        add(outs[0])


def products(info, groups, mine, sibling, before=None, ws=(0, 1), flat=True):
    width, cols = mine[0].shape
    plan, pieces = [], []
    for dx, group in groups:
        row, spans = 0, []
        for piece, start, length in group:
            spans.append((row, start, length))
            row += length
            pieces.append(piece)
        plan.append((dx, tuple(spans)))
    rows, steps = row, len(plan)
    anywhere = pl.BlockSpec(memory_space=pl.ANY)
    both = pl.BlockSpec((1, rows, cols), lambda n, info: (n // steps + ws[0], 0, 0))
    single = pl.BlockSpec((rows, cols), lambda n, info: (0, 0))
    args = [*pieces, *mine, *sibling]
    in_specs = [anywhere] * len(args)
    if before is not None:
        args.append(before)
        in_specs.append(both)
    return pl.pallas_call(
        functools.partial(products_kernel, plan=tuple(plan), first=before is None, ws=ws, flat=flat),
        grid_spec=pltpu.PrefetchScalarGridSpec(
            num_scalar_prefetch=1,
            grid=(len(ws) * steps,),
            in_specs=in_specs,
            out_specs=[single] * len(ws) if flat else both,
            scratch_shapes=[
                pltpu.VMEM((steps, rows, width), F32),
                pltpu.VMEM((steps, 2 * rows, width), BF16),
                pltpu.VMEM((2, width, cols), F32),
                pltpu.SemaphoreType.DMA((len(pieces),)),
                pltpu.SemaphoreType.DMA((2,)),
            ],
        ),
        out_shape=[jax.ShapeDtypeStruct((rows, cols), F32)] * len(ws)
        if flat
        else jax.ShapeDtypeStruct((2, rows, cols), F32),
        **params(name="products"),
    )(info, *args)


def finish_kernel(info, m0, m1, m2, m3, res, o_ref):
    total = (m0[...] + m1[...]) + (m2[...] + m3[...])
    lane = lax.broadcasted_iota(jnp.int32, (48, 128), 1)
    place = jnp.bitwise_and(lax.broadcasted_iota(jnp.int32, (48, 128), 0), 7)
    keep_a = lane < info[VIR + 2 * info[X] + info[C]]
    for n in range(2):
        rows = slice(48 * n, 48 * (n + 1))
        kept_b = info[VIR + 2 * pl.program_id(0) + n] - 8 * (4 * info[Y] + info[Z])
        keep = keep_a & (place < kept_b)
        for i in range(4):
            o_ref[i, rows, :] = res[i, rows, :] + jnp.where(keep, total[rows, 128 * i : 128 * (i + 1)], 0.0)


def finish(info, messages, residual):
    part = pl.BlockSpec((96, 512), lambda r, info: (r, 0))
    whole = pl.BlockSpec((4, 96, 128), lambda r, info: (0, r, 0))
    return pl.pallas_call(
        finish_kernel,
        grid_spec=pltpu.PrefetchScalarGridSpec(
            num_scalar_prefetch=1, grid=(4,), in_specs=[part] * 4 + [whole], out_specs=whole
        ),
        out_shape=jax.ShapeDtypeStruct(residual.shape, F32),
        **params(name="finish"),
    )(info, *messages, residual)


def tie_kernel(*refs):
    pass


def tie(value, *deps, cost=COST):
    anywhere = pl.BlockSpec(memory_space=pl.ANY)
    return pl.pallas_call(
        tie_kernel,
        in_specs=[anywhere] * (1 + len(deps)),
        out_specs=anywhere,
        out_shape=jax.ShapeDtypeStruct(value.shape, value.dtype),
        input_output_aliases={0: 0},
        cost_estimate=cost,
        name="tie",
    )(value, *deps)


def body(amplitudes, coupling, incoming_residual, occupied_count, virtual_count):
    kept = jnp.sum(virtual_count)
    branch = sum((kept > w).astype(jnp.int32) for w in WIDTHS[:-1])
    info = scalars(occupied_count, virtual_count)
    return lax.switch(
        branch,
        [functools.partial(packed_body, width=w) for w in WIDTHS],
        amplitudes,
        coupling,
        incoming_residual,
        info,
    )


def packed_body(amplitudes, coupling, incoming_residual, info, *, width):
    xi, ci = lax.axis_index("x"), lax.axis_index("c")

    amps = amplitudes.reshape(4, 2, 4, 128, 128)

    def at(by):
        return lax.dynamic_index_in_dim(amps, (xi + by) % 4, 0, keepdims=False)

    own, two_away = at(0), at(2)
    to_right = jnp.concatenate([at(1), two_away[:1]])
    to_left = jnp.concatenate([at(3), two_away[1:]])
    left, right = shift_x(to_right, 1), shift_x(to_left, -1)
    far0, far1 = shift_x(left[2:], 1), shift_x(right[2:], -1)

    def other(value):
        return lax.dynamic_index_in_dim(value, 1 - ci, 0, keepdims=False)

    sib = swap_core(jnp.stack([other(own), other(left), jnp.where(ci == 0, far1[0], far0[0]), other(right)]))

    packed = pack_b(info, coupling.reshape(-1, 128), to_right, width)
    blocks = [to_k_owner(p, u) for u, p in zip(ORDER, packed)]

    packed_a = pack_a(info, (own, left, right, far0, far1, sib), blocks[0], width)

    b0, b1 = tie(blocks[0], far0, far1), blocks[1]
    rows = b0.shape[0]
    mid = rows // 2
    left0, right0 = shift_x(b0, 1), shift_x(b0, -1)
    left1 = shift_x(jnp.concatenate([b1, left0[:mid]]), 1)
    right1 = shift_x(jnp.concatenate([b1, right0[mid:]]), -1)
    top = tie(left1[:mid], right1, cost=LONG)
    low = right1[mid:rows]
    left2, right2 = shift_x(top, 1), shift_x(low, -1)

    half = width // 2
    a_left, a_right = shift_y(packed_a, 1), shift_y(packed_a, -1)
    a_top = tie(a_left[:half], left0, right0)
    a_far = jnp.concatenate([shift_y(a_top, 1), shift_y(a_right[half:], -1)])
    a_far = tie(a_far, left1, right1)
    mine = (packed_a, a_left, a_right, a_far)
    sibling = tuple(swap_core(m) for m in mine)

    first = [
        (0, [(b0, 0, rows)]),
        (-1, [(left0, 0, rows)]),
        (1, [(right0, 0, rows)]),
        (2, [(left1, rows, mid), (right1, rows, mid)]),
    ]
    second = [(0, [(b1, 0, rows)]), (-1, [(left1, 0, rows)]), (1, [(right1, 0, rows)])]
    last = [(2, [(left2, 0, mid), (right2, 0, mid)])]
    sent0 = products(info, first, mine, sibling)
    acc = products(info, second, mine, sibling, flat=False)
    total = [to_home(sent0[w], ORDER[0], w) for w in range(2)]
    total += [to_home(products(info, last, mine, sibling, acc, (w,))[0], ORDER[1], w) for w in range(2)]
    return finish(info, total, incoming_residual.reshape(4, 384, 128)).reshape(incoming_residual.shape)


def solution(mesh):
    fine = Mesh(mesh.devices.reshape(NX, NC, NY, NZ), ("x", "c", "y", "z"))
    return jax.shard_map(
        body,
        mesh=fine,
        in_specs=(
            P(None, None, None, ("y", "z"), ("x", "c"), None),
            P(None, None, ("y", "z"), None, ("x", "c"), None),
            P(("x", "c"), None, None, None, ("y", "z"), None),
            P(),
            P(),
        ),
        out_specs=P(("x", "c"), None, None, None, ("y", "z"), None),
        check_vma=False,
    )
```

```python
import functools

import jax
import jax.numpy as jnp
from jax import lax
from jax.experimental import pallas as pl
from jax.experimental.pallas import tpu as pltpu
from jax.sharding import Mesh
from jax.sharding import PartitionSpec as P

NX, NC, NY, NZ = 4, 2, 4, 4
F32 = jnp.float32
BF16 = jnp.bfloat16
ORDER = (0, 1)
WIDTHS = (768, 896, 1024)
TILE = 256
COST = pl.CostEstimate(flops=1, bytes_accessed=1, transcendentals=0)
LONG = pl.CostEstimate(flops=2 * 10**10, bytes_accessed=7 * 10**7, transcendentals=0)


def split(x):
    hi = x.astype(BF16)
    lo = (x - hi.astype(F32)).astype(BF16)
    return hi, lo


VIR, OCC, X, C, Y, Z = 0, 8, 16, 17, 18, 19


def scalars(occupied_count, virtual_count):
    place = jnp.stack([lax.axis_index(n) for n in ("x", "c", "y", "z")])
    return jnp.concatenate([virtual_count, occupied_count, place]).astype(jnp.int32)


def params(mib, **more):
    return dict(compiler_params=pltpu.CompilerParams(vmem_limit_bytes=mib * 2**20), cost_estimate=COST, **more)


ROWS_B = 96


def pack_b_kernel(info, b_ref, after, *refs):
    outs, acc = refs[:2], refs[2]
    width = outs[0].shape[1]
    lane = lax.broadcasted_iota(jnp.int32, (ROWS_B, 128), 1)
    for u, o_ref in zip(ORDER, outs):
        e = jnp.bitwise_xor(jnp.bitwise_and(info[Z], 1), u)
        acc[...] = jnp.zeros_like(acc)

        def place(y, off):
            count = info[VIR + y]
            tile = off // 128
            start = off - tile * 128
            x = pltpu.roll(b_ref[pl.ds(2 * y + e, ROWS_B, stride=16), :], start, 1)
            here = pl.ds(pl.multiple_of(tile * 128, 128), 128)
            there = pl.ds(pl.multiple_of(tile * 128 + 128, 128), 128)
            acc[:, here] += jnp.where((lane >= start) & (lane < start + count), x, 0.0)
            acc[:, there] += jnp.where(lane < start + count - 128, x, 0.0)
            return off + count

        lax.fori_loop(0, 8, place, 0)
        o_ref[...] = acc[:, :width]


def pack_b(info, b2, after, width):
    rows = b2.shape[0] // 16
    out = pl.BlockSpec((ROWS_B, width), lambda r, info: (r, 0))
    return pl.pallas_call(
        pack_b_kernel,
        grid_spec=pltpu.PrefetchScalarGridSpec(
            num_scalar_prefetch=1,
            grid=(rows // ROWS_B,),
            in_specs=[
                pl.BlockSpec((ROWS_B * 16, 128), lambda r, info: (r, 0)),
                pl.BlockSpec(memory_space=pl.ANY),
            ],
            out_specs=[out, out],
            scratch_shapes=[pltpu.VMEM((ROWS_B, width + 256), F32)],
        ),
        out_shape=[jax.ShapeDtypeStruct((rows, width), F32)] * 2,
        **params(12, name="pack_coupling"),
    )(info, b2, after)


def pack_a_kernel(info, own, left, right, far0, far1, sib, after, o_ref, acc):
    width = o_ref.shape[0]
    acc[...] = jnp.zeros_like(acc)
    row = lax.broadcasted_iota(jnp.int32, (24, 128), 0)
    k = 4 * info[Y] + info[Z]
    core = info[C]
    for s in range(4):
        for cr in range(2):
            first = 32 * jnp.bitwise_and(info[X] + 4 - s, 3) + 16 * jnp.bitwise_xor(core, cr)

            def place(y, off, s=s, cr=cr, first=first):
                valid = jnp.where(k < info[OCC + y], info[VIR + y] - first, 0)
                base = off // 8 * 8
                start = off - base
                at = pl.ds(pl.multiple_of(jnp.minimum(base, width), 8), 24)
                mine = (row >= start) & (row < start + jnp.minimum(valid, 16))
                here = pl.ds(pl.multiple_of(16 * y, 16), 16)
                for i in range(4):
                    cols = slice(i * 128, (i + 1) * 128)
                    if cr == 1:
                        x = sib[s, i, here, :]
                    elif s == 2:
                        x = jnp.where(core == 0, far0[0, i, here, :], far1[0, i, here, :])
                    else:
                        x = (own, left, None, right)[s][core, i, here, :]
                    x = jnp.pad(x, ((0, 8), (0, 0)))
                    acc[at, cols] = jnp.where(mine, pltpu.roll(x, start, 0), acc[at, cols])
                return off + info[VIR + y]

            lax.fori_loop(0, 8, place, first)

    o_ref[...] = acc[: o_ref.shape[0], :]


def pack_a(info, parts, after, width):
    full = [pl.BlockSpec(p.shape, lambda i, info: (0, 0, 0, 0)) for p in parts]
    return pl.pallas_call(
        pack_a_kernel,
        grid_spec=pltpu.PrefetchScalarGridSpec(
            num_scalar_prefetch=1,
            grid=(1,),
            in_specs=full + [pl.BlockSpec(memory_space=pl.ANY)],
            out_specs=pl.BlockSpec((width, 512), lambda i, info: (0, 0)),
            scratch_shapes=[pltpu.VMEM((width + 24, 512), F32)],
        ),
        out_shape=jax.ShapeDtypeStruct((width, 512), F32),
        **params(16, name="pack_amplitudes"),
    )(info, *parts, after)


def permute(value, axes, pairs, name):
    with jax.named_scope(name):
        return lax.ppermute(value, axes, pairs)


def shift_y(value, by, name):
    return permute(value, "y", [(p, (p + by) % NY) for p in range(NY)], name)


def shift_x(value, by, name):
    return permute(value, "x", [(p, (p + by) % NX) for p in range(NX)], name)


def swap_core(value, name):
    return permute(value, "c", [(0, 1), (1, 0)], name)


def to_k_owner(value, u, name):
    pairs = []
    for c in range(NC):
        for z in range(NZ):
            pairs.append((c * NZ + z, (z // 2) * NZ + 2 * c + ((z % 2) ^ u)))
    return permute(value, ("c", "z"), pairs, name)


def to_home(value, w, name):
    pairs = []
    for c in range(NC):
        for z in range(NZ):
            pairs.append((c * NZ + z, ((z // 2) ^ w) * NZ + 2 * c + ((z % 2) ^ 1)))
    return permute(value, ("c", "z"), pairs, name)


def to_relay(value0, value1, name):
    first, second = [], []
    for c in range(NC):
        for z in range(NZ):
            at, other = c * NZ + z, 1 if z % 2 == 0 else -1
            if z // 2 == c:
                second.append((at, (1 - c) * NZ + z))
            else:
                first.append((at, c * NZ + (z + other) % NZ))
                second.append((at, c * NZ + (z - other) % NZ))
    return permute(value0, ("c", "z"), first, name), permute(value1, ("c", "z"), second, name)


def products_kernel(info, *refs, plan, first, ws, flat, phase, relayed):
    blocks = 3 if phase == 1 else 4
    refs = refs[1:]
    count = sum(len(g[1]) for g in plan)
    pieces, a_refs, refs = refs[:count], (refs[count : count + blocks], refs[count + blocks : count + 2 * blocks]), refs[count + 2 * blocks :]
    if not first:
        before, refs = refs[0], refs[1:]
    if relayed:
        relay0, relay1, refs = refs[0], refs[1], refs[2:]
    outs, (b_f32, b_both, a_buf, acc, b_sem, a_sem) = refs[:-6], refs[-6:]
    steps = len(plan)
    n = pl.program_id(0)
    w = n // steps
    t = n - w * steps
    rows_all = b_f32.shape[1]

    def away_y(t):
        dx = plan[0][0]
        for at, (other, _) in enumerate(plan[1:]):
            dx = jnp.where(t == at + 1, other, dx)
        return dx, jnp.bitwise_and(info[X] + dx + 4 - info[Y], 3)

    def active(n):
        dx, d = away_y(n - n // steps * steps)
        if phase == 1:
            return d != 2
        if phase == 2:
            return (dx == 2) | (d == 2)
        return n >= 0

    def fetch_a(n, slot):
        w = n // steps
        _, d = away_y(n - w * steps)
        sibling = jnp.bitwise_xor(jnp.bitwise_xor(info[Z] // 2, w + ws[0]), info[C])
        for m, blocks in enumerate(a_refs):
            for way, ref in zip((0, 3, 1, 2), blocks):

                @pl.when((sibling == m) & (d == way))
                def _(ref=ref):
                    for part in range(4):
                        rows = pl.ds(part * (a_buf.shape[1] // 4), a_buf.shape[1] // 4)
                        pltpu.make_async_copy(ref.at[rows], a_buf.at[slot, rows], a_sem.at[slot]).start()

    def b_copies(t):
        at = sum(len(g[1]) for g in plan[:t])
        return [
            pltpu.make_async_copy(pieces[at + p].at[pl.ds(start, rows)], b_f32.at[t, pl.ds(row, rows)], b_sem.at[at + p])
            for p, (row, start, rows) in enumerate(plan[t][1])
        ]

    @pl.when(n == 0)
    def _():
        pl.when(active(0))(lambda: fetch_a(0, 0))
        for t in range(steps):

            @pl.when(active(t))
            def _(t=t):
                for copy in b_copies(t):
                    copy.start()

    @pl.when((n + 1 < len(ws) * steps) & active(n + 1))
    def _():
        fetch_a(n + 1, (n + 1) % 2)

    for at in range(steps):

        @pl.when((n == at) & active(at))
        def _(at=at):
            for copy in b_copies(at):
                copy.wait()
            hi, lo = split(b_f32[at])
            b_both[at, :rows_all, :] = hi
            b_both[at, rows_all:, :] = lo

    @pl.when(t == 0)
    def _():
        acc[...] = jnp.zeros_like(acc) if first else before[...].reshape(acc.shape)

    if relayed:

        @pl.when(n == 0)
        def _():
            acc[...] += jnp.where(info[C] != info[Z] // 2, relay0[...], relay1[...])

    @pl.when(active(n))
    def _():
        slot = n % 2
        pltpu.make_async_copy(a_refs[0][0], a_buf.at[slot], a_sem.at[slot]).wait()

        a_hi, a_lo = split(a_buf[slot])
        new = jnp.dot(b_both[t], a_hi, preferred_element_type=F32)
        acc[...] += new[:rows_all] + new[rows_all:] + jnp.dot(b_both[t, :rows_all, :], a_lo, preferred_element_type=F32)

    for at in range(len(ws)):

        @pl.when(n == (at + 1) * steps - 1)
        def _(at=at):
            if flat:
                outs[at][...] = acc[...]
            else:
                outs[0][0] = acc[...]


def products(info, after, groups, mine, sibling, before=None, ws=(0, 1), flat=True, phase=0, relay=()):
    width, cols = mine[0].shape
    plan, pieces = [], []
    for dx, group in groups:
        row, spans = 0, []
        for piece, start, length in group:
            spans.append((row, start, length))
            row += length
            pieces.append(piece)
        plan.append((dx, tuple(spans)))
    rows, steps = row, len(plan)
    anywhere = pl.BlockSpec(memory_space=pl.ANY)
    both = pl.BlockSpec((1, rows, cols), lambda n, info: (n // steps + ws[0], 0, 0))
    single = pl.BlockSpec((rows, cols), lambda n, info: (0, 0))
    args = [after, *pieces, *mine, *sibling]
    in_specs = [anywhere] * len(args)
    if before is not None:
        args.append(before)
        in_specs.append(both)
    args += relay
    in_specs += [single] * len(relay)
    return pl.pallas_call(
        functools.partial(products_kernel, plan=tuple(plan), first=before is None, ws=ws, flat=flat, phase=phase, relayed=bool(relay)),
        grid_spec=pltpu.PrefetchScalarGridSpec(
            num_scalar_prefetch=1,
            grid=(len(ws) * steps,),
            in_specs=in_specs,
            out_specs=[single] * len(ws) if flat else both,
            scratch_shapes=[
                pltpu.VMEM((steps, rows, width), F32),
                pltpu.VMEM((steps, 2 * rows, width), BF16),
                pltpu.VMEM((2, width, cols), F32),
                pltpu.VMEM((rows, cols), F32),
                pltpu.SemaphoreType.DMA((len(pieces),)),
                pltpu.SemaphoreType.DMA((2,)),
            ],
        ),
        out_shape=[jax.ShapeDtypeStruct((rows, cols), F32)] * len(ws)
        if flat
        else jax.ShapeDtypeStruct((2, rows, cols), F32),
        **params(30, name="products"),
    )(info, *args)


def finish_kernel(info, stayed, came, m2, m3, res, o_ref):
    total = jnp.where(info[C] != info[Z] // 2, came[...], stayed[...]) + (m2[...] + m3[...])
    lane = lax.broadcasted_iota(jnp.int32, (48, 128), 1)
    place = jnp.bitwise_and(lax.broadcasted_iota(jnp.int32, (48, 128), 0), 7)
    keep_a = lane < info[VIR + 2 * info[X] + info[C]]
    for g in range(8):
        rows = slice(48 * g, 48 * (g + 1))
        keep = keep_a & (place < info[VIR + g] - 8 * (4 * info[Y] + info[Z]))
        o_ref[0, rows, :] = res[0, rows, :] + jnp.where(keep, total[rows], 0.0)


def finish(info, messages, residual):
    rows = residual.shape[1]
    part = pl.BlockSpec((rows, 128), lambda i, info: (0, i))
    whole = pl.BlockSpec((1, rows, 128), lambda i, info: (i, 0, 0))
    return pl.pallas_call(
        finish_kernel,
        grid_spec=pltpu.PrefetchScalarGridSpec(
            num_scalar_prefetch=1, grid=(4,), in_specs=[part] * 4 + [whole], out_specs=whole
        ),
        out_shape=jax.ShapeDtypeStruct(residual.shape, F32),
        **params(10, name="finish"),
    )(info, *messages, residual)


def tie(value, *deps, cost=COST):
    anywhere = pl.BlockSpec(memory_space=pl.ANY)
    return pl.pallas_call(
        stage_kernel,
        in_specs=[anywhere] * (1 + len(deps)),
        out_specs=anywhere,
        out_shape=jax.ShapeDtypeStruct(value.shape, value.dtype),
        input_output_aliases={0: 0},
        cost_estimate=cost,
        name="tie",
    )(value, *deps)


def stage_kernel(*refs):
    pass


def stage(*values):
    anywhere = pl.BlockSpec(memory_space=pl.ANY)
    return pl.pallas_call(
        stage_kernel,
        in_specs=[anywhere] * len(values),
        out_specs=[anywhere] * len(values),
        out_shape=[jax.ShapeDtypeStruct(v.shape, v.dtype) for v in values],
        input_output_aliases={n: n for n in range(len(values))},
        cost_estimate=COST,
        name="stage",
    )(*values)


def body(amplitudes, coupling, incoming_residual, occupied_count, virtual_count):
    kept = jnp.sum(virtual_count)
    branch = sum((kept > w).astype(jnp.int32) for w in WIDTHS[:-1])
    info = scalars(occupied_count, virtual_count)
    return lax.switch(
        branch,
        [functools.partial(packed_body, width=w) for w in WIDTHS],
        amplitudes,
        coupling,
        incoming_residual,
        info,
    )


def packed_body(amplitudes, coupling, incoming_residual, info, *, width):
    xi, ci = lax.axis_index("x"), lax.axis_index("c")

    amps = amplitudes.reshape(4, 2, 4, 128, 128)

    def at(by):
        return lax.dynamic_index_in_dim(amps, (xi + by) % 4, 0, keepdims=False)

    own, two_away = at(0), at(2)
    to_right = jnp.concatenate([at(1), two_away[:1]])
    to_left = jnp.concatenate([at(3), two_away[1:]])
    left, right = shift_x(to_right, 1, "amps_left"), shift_x(to_left, -1, "amps_right")
    packed = pack_b(info, coupling.reshape(-1, 128), to_right, width)
    via_left, via_right = left[2:], right[2:]
    via_left, via_right, p0, p1 = stage(via_left, via_right, *packed)
    far0, far1 = shift_x(via_left, 1, "amps_far0"), shift_x(via_right, -1, "amps_far1")
    b0, b1 = (to_k_owner(p, u, "coupling_to_k") for u, p in zip(ORDER, (p0, p1)))

    def other(value):
        return lax.dynamic_index_in_dim(value, 1 - ci, 0, keepdims=False)

    sib = swap_core(
        jnp.stack([other(own), other(left), jnp.where(ci == 0, far1[0], far0[0]), other(right)]), "amps_sibling"
    )
    packed_a = pack_a(info, (own, left, right, far0, far1, sib), p0, width)

    rows = b0.shape[0]
    mid = rows // 2
    b0, _, _ = stage(b0, far0, far1)
    left0, right0 = shift_x(b0, 1, "b0_left"), shift_x(b0, -1, "b0_right")
    left1 = shift_x(jnp.concatenate([b1, left0[:mid]]), 1, "b1_left")
    right1 = shift_x(jnp.concatenate([b1, right0[mid:]]), -1, "b1_right")
    top = tie(left1[:mid], right1, cost=LONG)
    left2 = shift_x(top, 1, "b2_left")
    right2 = shift_x(right1[mid:rows], -1, "b2_right")

    half = width // 2
    a_left, a_right = shift_y(packed_a, 1, "a_left"), shift_y(packed_a, -1, "a_right")
    a_top = tie(a_left[:half], left0, right0)
    a_far = jnp.concatenate([shift_y(a_top, 1, "a_top"), shift_y(a_right[half:], -1, "a_low")])
    mine = (packed_a, a_left, a_right, a_far)
    sibling = tuple(swap_core(m, "a_sibling") for m in mine)

    near0 = [(0, [(b0, 0, rows)]), (-1, [(left0, 0, rows)]), (1, [(right0, 0, rows)])]
    far0 = [(2, [(left1, rows, mid), (right1, rows, mid)])]
    near1 = [(0, [(b1, 0, rows)]), (-1, [(left1, 0, rows)]), (1, [(right1, 0, rows)])]
    far1 = [(2, [(left2, 0, mid), (right2, 0, mid)])]
    sent0 = products(info, top, near0 + far0, mine, sibling)
    acc1 = products(info, sent0[0], near1, mine, sibling, flat=False)
    relay = to_relay(*sent0, "home0")
    sent1 = products(info, acc1, far1, mine, sibling, acc1, relay=relay)
    total = [sent0[0], relay[1], *(to_home(sent1[w], w, "home1") for w in range(2))]
    return finish(info, total, incoming_residual.reshape(4, 384, 128)).reshape(incoming_residual.shape)


def solution(mesh):
    fine = Mesh(mesh.devices.reshape(NX, NC, NY, NZ), ("x", "c", "y", "z"))
    return jax.shard_map(
        body,
        mesh=fine,
        in_specs=(
            P(None, None, None, ("y", "z"), ("x", "c"), None),
            P(None, None, ("y", "z"), None, ("x", "c"), None),
            P(("x", "c"), None, None, None, ("y", "z"), None),
            P(),
            P(),
        ),
        out_specs=P(("x", "c"), None, None, None, ("y", "z"), None),
        check_vma=False,
    )
```

```python
import functools

import jax
import jax.numpy as jnp
from jax import lax
from jax.experimental import pallas as pl
from jax.experimental.pallas import tpu as pltpu
from jax.sharding import Mesh
from jax.sharding import PartitionSpec as P

NX, NC, NY, NZ = 4, 2, 4, 4
F32 = jnp.float32
BF16 = jnp.bfloat16
ORDER = (0, 1)
WIDTHS = (768, 896)
TILE = 256
COST = pl.CostEstimate(flops=1, bytes_accessed=1, transcendentals=0)
LONG = pl.CostEstimate(flops=2 * 10**10, bytes_accessed=7 * 10**7, transcendentals=0)


def split(x):
    hi = x.astype(BF16)
    lo = (x - hi.astype(F32)).astype(BF16)
    return hi, lo


VIR, OCC, X, C, Y, Z, PASS = 0, 8, 16, 17, 18, 19, 20


def scalars(occupied_count, virtual_count):
    place = jnp.stack([lax.axis_index(n) for n in ("x", "c", "y", "z")])
    return jnp.concatenate([virtual_count, occupied_count, place]).astype(jnp.int32)


def params(mib, **more):
    return dict(compiler_params=pltpu.CompilerParams(vmem_limit_bytes=mib * 2**20), cost_estimate=COST, **more)


ROWS_B = 96


def pack_b_kernel(info, b_ref, after, *refs):
    outs, acc = refs[:2], refs[2]
    width = outs[0].shape[1]
    lane = lax.broadcasted_iota(jnp.int32, (ROWS_B, 128), 1)
    for u, o_ref in zip(ORDER, outs):
        e = jnp.bitwise_xor(jnp.bitwise_and(info[Z], 1), u)
        acc[...] = jnp.zeros_like(acc)

        def place(y, off):
            count = info[VIR + y]
            tile = off // 128
            start = off - tile * 128
            tile = jnp.clip(tile - info[PASS] * (width // 128) + 2, 0, width // 128 + 2)
            x = pltpu.roll(b_ref[pl.ds(2 * y + e, ROWS_B, stride=16), :], start, 1)
            here = pl.ds(pl.multiple_of(tile * 128, 128), 128)
            there = pl.ds(pl.multiple_of(tile * 128 + 128, 128), 128)
            acc[:, here] += jnp.where((lane >= start) & (lane < start + count), x, 0.0)
            acc[:, there] += jnp.where(lane < start + count - 128, x, 0.0)
            return off + count

        lax.fori_loop(0, 8, place, 0)
        o_ref[...] = acc[:, 256 : 256 + width]


def pack_b(info, b2, after, width):
    rows = b2.shape[0] // 16
    out = pl.BlockSpec((ROWS_B, width), lambda r, info: (r, 0))
    return pl.pallas_call(
        pack_b_kernel,
        grid_spec=pltpu.PrefetchScalarGridSpec(
            num_scalar_prefetch=1,
            grid=(rows // ROWS_B,),
            in_specs=[
                pl.BlockSpec((ROWS_B * 16, 128), lambda r, info: (r, 0)),
                pl.BlockSpec(memory_space=pl.ANY),
            ],
            out_specs=[out, out],
            scratch_shapes=[pltpu.VMEM((ROWS_B, width + 512), F32)],
        ),
        out_shape=[jax.ShapeDtypeStruct((rows, width), F32)] * 2,
        **params(12, name="pack_coupling"),
    )(info, b2, after)


def pack_a_kernel(info, own, left, right, far0, far1, sib, after, o_ref, acc):
    width = o_ref.shape[0]
    acc[...] = jnp.zeros_like(acc)
    row = lax.broadcasted_iota(jnp.int32, (24, 128), 0)
    k = 4 * info[Y] + info[Z]
    core = info[C]
    for s in range(4):
        for cr in range(2):
            first = 32 * jnp.bitwise_and(info[X] + 4 - s, 3) + 16 * jnp.bitwise_xor(core, cr)

            def place(y, off, s=s, cr=cr, first=first):
                valid = jnp.where(k < info[OCC + y], info[VIR + y] - first, 0)
                base = off // 8 * 8
                start = off - base
                base = jnp.clip(base - info[PASS] * width + 24, 0, width + 24)
                at = pl.ds(pl.multiple_of(base, 8), 24)
                mine = (row >= start) & (row < start + jnp.minimum(valid, 16))
                here = pl.ds(pl.multiple_of(16 * y, 16), 16)
                for i in range(4):
                    cols = slice(i * 128, (i + 1) * 128)
                    if cr == 1:
                        x = sib[s, i, here, :]
                    elif s == 2:
                        x = jnp.where(core == 0, far0[0, i, here, :], far1[0, i, here, :])
                    else:
                        x = (own, left, None, right)[s][core, i, here, :]
                    x = jnp.pad(x, ((0, 8), (0, 0)))
                    acc[at, cols] = jnp.where(mine, pltpu.roll(x, start, 0), acc[at, cols])
                return off + info[VIR + y]

            lax.fori_loop(0, 8, place, first)

    o_ref[...] = acc[24 : 24 + width, :]


def pack_a(info, parts, after, width):
    full = [pl.BlockSpec(p.shape, lambda i, info: (0, 0, 0, 0)) for p in parts]
    return pl.pallas_call(
        pack_a_kernel,
        grid_spec=pltpu.PrefetchScalarGridSpec(
            num_scalar_prefetch=1,
            grid=(1,),
            in_specs=full + [pl.BlockSpec(memory_space=pl.ANY)],
            out_specs=pl.BlockSpec((width, 512), lambda i, info: (0, 0)),
            scratch_shapes=[pltpu.VMEM((width + 48, 512), F32)],
        ),
        out_shape=jax.ShapeDtypeStruct((width, 512), F32),
        **params(16, name="pack_amplitudes"),
    )(info, *parts, after)


def permute(value, axes, pairs, name):
    with jax.named_scope(name):
        return lax.ppermute(value, axes, pairs)


def shift_y(value, by, name):
    return permute(value, "y", [(p, (p + by) % NY) for p in range(NY)], name)


def shift_x(value, by, name):
    return permute(value, "x", [(p, (p + by) % NX) for p in range(NX)], name)


def swap_core(value, name):
    return permute(value, "c", [(0, 1), (1, 0)], name)


def to_k_owner(value, u, name):
    pairs = []
    for c in range(NC):
        for z in range(NZ):
            pairs.append((c * NZ + z, (z // 2) * NZ + 2 * c + ((z % 2) ^ u)))
    return permute(value, ("c", "z"), pairs, name)


def to_home(value, w, name):
    pairs = []
    for c in range(NC):
        for z in range(NZ):
            pairs.append((c * NZ + z, ((z // 2) ^ w) * NZ + 2 * c + ((z % 2) ^ 1)))
    return permute(value, ("c", "z"), pairs, name)


def to_relay(value0, value1, name):
    first, second = [], []
    for c in range(NC):
        for z in range(NZ):
            at, other = c * NZ + z, 1 if z % 2 == 0 else -1
            if z // 2 == c:
                second.append((at, (1 - c) * NZ + z))
            else:
                first.append((at, c * NZ + (z + other) % NZ))
                second.append((at, c * NZ + (z - other) % NZ))
    return permute(value0, ("c", "z"), first, name), permute(value1, ("c", "z"), second, name)


def products_kernel(info, *refs, plan, first, ws, flat, phase, relayed):
    blocks = 3 if phase == 1 else 4
    refs = refs[1:]
    count = sum(len(g[1]) for g in plan)
    pieces, a_refs, refs = refs[:count], (refs[count : count + blocks], refs[count + blocks : count + 2 * blocks]), refs[count + 2 * blocks :]
    if not first:
        before, refs = refs[0], refs[1:]
    if relayed:
        relay0, relay1, refs = refs[0], refs[1], refs[2:]
    outs, (b_f32, b_both, a_buf, acc, b_sem, a_sem) = refs[:-6], refs[-6:]
    steps = len(plan)
    n = pl.program_id(0)
    w = n // steps
    t = n - w * steps
    rows_all = b_f32.shape[1]

    def away_y(t):
        dx = plan[0][0]
        for at, (other, _) in enumerate(plan[1:]):
            dx = jnp.where(t == at + 1, other, dx)
        return dx, jnp.bitwise_and(info[X] + dx + 4 - info[Y], 3)

    def active(n):
        dx, d = away_y(n - n // steps * steps)
        if phase == 1:
            return d != 2
        if phase == 2:
            return (dx == 2) | (d == 2)
        return n >= 0

    def fetch_a(n, slot):
        w = n // steps
        _, d = away_y(n - w * steps)
        sibling = jnp.bitwise_xor(jnp.bitwise_xor(info[Z] // 2, w + ws[0]), info[C])
        for m, blocks in enumerate(a_refs):
            for way, ref in zip((0, 3, 1, 2), blocks):

                @pl.when((sibling == m) & (d == way))
                def _(ref=ref):
                    for part in range(4):
                        rows = pl.ds(part * (a_buf.shape[1] // 4), a_buf.shape[1] // 4)
                        pltpu.make_async_copy(ref.at[rows], a_buf.at[slot, rows], a_sem.at[slot]).start()

    def b_copies(t):
        at = sum(len(g[1]) for g in plan[:t])
        return [
            pltpu.make_async_copy(pieces[at + p].at[pl.ds(start, rows)], b_f32.at[t, pl.ds(row, rows)], b_sem.at[at + p])
            for p, (row, start, rows) in enumerate(plan[t][1])
        ]

    @pl.when(n == 0)
    def _():
        pl.when(active(0))(lambda: fetch_a(0, 0))
        for t in range(steps):

            @pl.when(active(t))
            def _(t=t):
                for copy in b_copies(t):
                    copy.start()

    @pl.when((n + 1 < len(ws) * steps) & active(n + 1))
    def _():
        fetch_a(n + 1, (n + 1) % 2)

    for at in range(steps):

        @pl.when((n == at) & active(at))
        def _(at=at):
            for copy in b_copies(at):
                copy.wait()
            hi, lo = split(b_f32[at])
            b_both[at, :rows_all, :] = hi
            b_both[at, rows_all:, :] = lo

    @pl.when(t == 0)
    def _():
        acc[...] = jnp.zeros_like(acc) if first else before[...].reshape(acc.shape)

    if relayed:

        @pl.when(n == 0)
        def _():
            acc[...] += jnp.where(info[C] != info[Z] // 2, relay0[...], relay1[...])

    @pl.when(active(n))
    def _():
        slot = n % 2
        pltpu.make_async_copy(a_refs[0][0], a_buf.at[slot], a_sem.at[slot]).wait()

        a_hi, a_lo = split(a_buf[slot])
        new = jnp.dot(b_both[t], a_hi, preferred_element_type=F32)
        acc[...] += new[:rows_all] + new[rows_all:] + jnp.dot(b_both[t, :rows_all, :], a_lo, preferred_element_type=F32)

    for at in range(len(ws)):

        @pl.when(n == (at + 1) * steps - 1)
        def _(at=at):
            if flat:
                outs[at][...] = acc[...]
            else:
                outs[0][0] = acc[...]


def products(info, after, groups, mine, sibling, before=None, ws=(0, 1), flat=True, phase=0, relay=()):
    width, cols = mine[0].shape
    plan, pieces = [], []
    for dx, group in groups:
        row, spans = 0, []
        for piece, start, length in group:
            spans.append((row, start, length))
            row += length
            pieces.append(piece)
        plan.append((dx, tuple(spans)))
    rows, steps = row, len(plan)
    anywhere = pl.BlockSpec(memory_space=pl.ANY)
    both = pl.BlockSpec((1, rows, cols), lambda n, info: (n // steps + ws[0], 0, 0))
    single = pl.BlockSpec((rows, cols), lambda n, info: (0, 0))
    args = [after, *pieces, *mine, *sibling]
    in_specs = [anywhere] * len(args)
    if before is not None:
        args.append(before)
        in_specs.append(both)
    args += relay
    in_specs += [single] * len(relay)
    return pl.pallas_call(
        functools.partial(products_kernel, plan=tuple(plan), first=before is None, ws=ws, flat=flat, phase=phase, relayed=bool(relay)),
        grid_spec=pltpu.PrefetchScalarGridSpec(
            num_scalar_prefetch=1,
            grid=(len(ws) * steps,),
            in_specs=in_specs,
            out_specs=[single] * len(ws) if flat else both,
            scratch_shapes=[
                pltpu.VMEM((steps, rows, width), F32),
                pltpu.VMEM((steps, 2 * rows, width), BF16),
                pltpu.VMEM((2, width, cols), F32),
                pltpu.VMEM((rows, cols), F32),
                pltpu.SemaphoreType.DMA((len(pieces),)),
                pltpu.SemaphoreType.DMA((2,)),
            ],
        ),
        out_shape=[jax.ShapeDtypeStruct((rows, cols), F32)] * len(ws)
        if flat
        else jax.ShapeDtypeStruct((2, rows, cols), F32),
        **params(30, name="products"),
    )(info, *args)


def finish_kernel(info, stayed, came, m2, m3, res, o_ref):
    total = jnp.where(info[C] != info[Z] // 2, came[...], stayed[...]) + (m2[...] + m3[...])
    lane = lax.broadcasted_iota(jnp.int32, (48, 128), 1)
    place = jnp.bitwise_and(lax.broadcasted_iota(jnp.int32, (48, 128), 0), 7)
    keep_a = lane < info[VIR + 2 * info[X] + info[C]]
    for g in range(8):
        rows = slice(48 * g, 48 * (g + 1))
        keep = keep_a & (place < info[VIR + g] - 8 * (4 * info[Y] + info[Z]))
        o_ref[0, rows, :] = res[0, rows, :] + jnp.where(keep, total[rows], 0.0)


def finish(info, messages, residual):
    rows = residual.shape[1]
    part = pl.BlockSpec((rows, 128), lambda i, info: (0, i))
    whole = pl.BlockSpec((1, rows, 128), lambda i, info: (i, 0, 0))
    return pl.pallas_call(
        finish_kernel,
        grid_spec=pltpu.PrefetchScalarGridSpec(
            num_scalar_prefetch=1, grid=(4,), in_specs=[part] * 4 + [whole], out_specs=whole
        ),
        out_shape=jax.ShapeDtypeStruct(residual.shape, F32),
        **params(10, name="finish"),
    )(info, *messages, residual)


def tie(value, *deps, cost=COST):
    anywhere = pl.BlockSpec(memory_space=pl.ANY)
    return pl.pallas_call(
        stage_kernel,
        in_specs=[anywhere] * (1 + len(deps)),
        out_specs=anywhere,
        out_shape=jax.ShapeDtypeStruct(value.shape, value.dtype),
        input_output_aliases={0: 0},
        cost_estimate=cost,
        name="tie",
    )(value, *deps)


def stage_kernel(*refs):
    pass


def stage(*values):
    anywhere = pl.BlockSpec(memory_space=pl.ANY)
    return pl.pallas_call(
        stage_kernel,
        in_specs=[anywhere] * len(values),
        out_specs=[anywhere] * len(values),
        out_shape=[jax.ShapeDtypeStruct(v.shape, v.dtype) for v in values],
        input_output_aliases={n: n for n in range(len(values))},
        cost_estimate=COST,
        name="stage",
    )(*values)


def body(amplitudes, coupling, incoming_residual, occupied_count, virtual_count):
    kept = jnp.sum(virtual_count)
    narrow, wide = WIDTHS
    info = scalars(occupied_count, virtual_count)

    amps = amplitudes.reshape(4, 2, 4, 128, 128)
    coupling_rows = coupling.reshape(-1, 128)

    def one(width, n, residual):
        numbered = jnp.concatenate([info, jnp.full((1,), n, jnp.int32)])
        return packed_body(amps, coupling_rows, residual, numbered, width=width)

    return lax.cond(
        kept <= narrow,
        lambda residual: one(narrow, 0, residual),
        lambda residual: lax.fori_loop(0, (kept + wide - 1) // wide, functools.partial(one, wide), residual),
        incoming_residual,
    )


def packed_body(amps, coupling_rows, incoming_residual, info, *, width):
    xi, ci = lax.axis_index("x"), lax.axis_index("c")

    def at(by):
        return lax.dynamic_index_in_dim(amps, (xi + by) % 4, 0, keepdims=False)

    own, two_away = at(0), at(2)
    to_right = jnp.concatenate([at(1), two_away[:1]])
    to_left = jnp.concatenate([at(3), two_away[1:]])
    left, right = shift_x(to_right, 1, "amps_left"), shift_x(to_left, -1, "amps_right")
    packed = pack_b(info, coupling_rows, to_right, width)
    via_left, via_right = left[2:], right[2:]
    via_left, via_right, p0, p1 = stage(via_left, via_right, *packed)
    far0, far1 = shift_x(via_left, 1, "amps_far0"), shift_x(via_right, -1, "amps_far1")
    b0, b1 = (to_k_owner(p, u, "coupling_to_k") for u, p in zip(ORDER, (p0, p1)))

    def other(value):
        return lax.dynamic_index_in_dim(value, 1 - ci, 0, keepdims=False)

    sib = swap_core(
        jnp.stack([other(own), other(left), jnp.where(ci == 0, far1[0], far0[0]), other(right)]), "amps_sibling"
    )
    packed_a = pack_a(info, (own, left, right, far0, far1, sib), p0, width)

    rows = b0.shape[0]
    mid = rows // 2
    b0, _, _ = stage(b0, far0, far1)
    left0, right0 = shift_x(b0, 1, "b0_left"), shift_x(b0, -1, "b0_right")
    left1 = shift_x(jnp.concatenate([b1, left0[:mid]]), 1, "b1_left")
    right1 = shift_x(jnp.concatenate([b1, right0[mid:]]), -1, "b1_right")
    top = tie(left1[:mid], right1, cost=LONG)
    left2 = shift_x(top, 1, "b2_left")
    right2 = shift_x(right1[mid:rows], -1, "b2_right")

    half = width // 2
    a_left, a_right = shift_y(packed_a, 1, "a_left"), shift_y(packed_a, -1, "a_right")
    a_top = tie(a_left[:half], left0, right0)
    a_far = jnp.concatenate([shift_y(a_top, 1, "a_top"), shift_y(a_right[half:], -1, "a_low")])
    mine = (packed_a, a_left, a_right, a_far)
    sibling = tuple(swap_core(m, "a_sibling") for m in mine)

    near0 = [(0, [(b0, 0, rows)]), (-1, [(left0, 0, rows)]), (1, [(right0, 0, rows)])]
    far0 = [(2, [(left1, rows, mid), (right1, rows, mid)])]
    near1 = [(0, [(b1, 0, rows)]), (-1, [(left1, 0, rows)]), (1, [(right1, 0, rows)])]
    far1 = [(2, [(left2, 0, mid), (right2, 0, mid)])]
    sent0 = products(info, top, near0 + far0, mine, sibling)
    acc1 = products(info, sent0[0], near1, mine, sibling, flat=False)
    relay = to_relay(*sent0, "home0")
    sent1 = products(info, acc1, far1, mine, sibling, acc1, relay=relay)
    total = [sent0[0], relay[1], *(to_home(sent1[w], w, "home1") for w in range(2))]
    return finish(info, total, incoming_residual.reshape(4, 384, 128)).reshape(incoming_residual.shape)


def solution(mesh):
    fine = Mesh(mesh.devices.reshape(NX, NC, NY, NZ), ("x", "c", "y", "z"))
    return jax.shard_map(
        body,
        mesh=fine,
        in_specs=(
            P(None, None, None, ("y", "z"), ("x", "c"), None),
            P(None, None, ("y", "z"), None, ("x", "c"), None),
            P(("x", "c"), None, None, None, ("y", "z"), None),
            P(),
            P(),
        ),
        out_specs=P(("x", "c"), None, None, None, ("y", "z"), None),
        check_vma=False,
    )
```

```python
import functools

import jax
import jax.numpy as jnp
from jax import lax
from jax.experimental import pallas as pl
from jax.experimental.pallas import tpu as pltpu
from jax.sharding import Mesh
from jax.sharding import PartitionSpec as P

NX, NC, NY, NZ = 4, 2, 4, 4
F32 = jnp.float32
BF16 = jnp.bfloat16
ORDER = (0, 1)
WIDTHS = (768, 896)
TILE = 256
COST = pl.CostEstimate(flops=1, bytes_accessed=1, transcendentals=0)
LONG = pl.CostEstimate(flops=2 * 10**10, bytes_accessed=7 * 10**7, transcendentals=0)


def split(x):
    hi = x.astype(BF16)
    lo = (x - hi.astype(F32)).astype(BF16)
    return hi, lo


VIR, OCC, X, C, Y, Z, PASS = 0, 8, 16, 17, 18, 19, 20


def scalars(occupied_count, virtual_count):
    place = jnp.stack([lax.axis_index(n) for n in ("x", "c", "y", "z")])
    return jnp.concatenate([virtual_count, occupied_count, place]).astype(jnp.int32)


def params(mib, **more):
    return dict(compiler_params=pltpu.CompilerParams(vmem_limit_bytes=mib * 2**20), cost_estimate=COST, **more)


ROWS_B = 96


def pack_b_kernel(info, b_ref, after, *refs):
    outs, acc = refs[:2], refs[2]
    width = outs[0].shape[1]
    lane = lax.broadcasted_iota(jnp.int32, (ROWS_B, 128), 1)
    for u, o_ref in zip(ORDER, outs):
        e = jnp.bitwise_xor(jnp.bitwise_and(info[Z], 1), u)
        acc[...] = jnp.zeros_like(acc)

        def place(y, off):
            count = info[VIR + y]
            tile = off // 128
            start = off - tile * 128
            tile = jnp.clip(tile - info[PASS] * (width // 128) + 2, 0, width // 128 + 2)
            x = pltpu.roll(b_ref[pl.ds(2 * y + e, ROWS_B, stride=16), :], start, 1)
            here = pl.ds(pl.multiple_of(tile * 128, 128), 128)
            there = pl.ds(pl.multiple_of(tile * 128 + 128, 128), 128)
            acc[:, here] += jnp.where((lane >= start) & (lane < start + count), x, 0.0)
            acc[:, there] += jnp.where(lane < start + count - 128, x, 0.0)
            return off + count

        lax.fori_loop(0, 8, place, 0)
        o_ref[...] = acc[:, 256 : 256 + width]


def pack_b(info, b2, after, width):
    rows = b2.shape[0] // 16
    out = pl.BlockSpec((ROWS_B, width), lambda r, info: (r, 0))
    return pl.pallas_call(
        pack_b_kernel,
        grid_spec=pltpu.PrefetchScalarGridSpec(
            num_scalar_prefetch=1,
            grid=(rows // ROWS_B,),
            in_specs=[
                pl.BlockSpec((ROWS_B * 16, 128), lambda r, info: (r, 0)),
                pl.BlockSpec(memory_space=pl.ANY),
            ],
            out_specs=[out, out],
            scratch_shapes=[pltpu.VMEM((ROWS_B, width + 512), F32)],
        ),
        out_shape=[jax.ShapeDtypeStruct((rows, width), F32)] * 2,
        **params(12, name="pack_coupling"),
    )(info, b2, after)


def pack_a_kernel(info, own, left, right, far0, far1, sib, after, o_ref, acc):
    width = o_ref.shape[0]
    acc[...] = jnp.zeros_like(acc)
    row = lax.broadcasted_iota(jnp.int32, (24, 128), 0)
    k = 4 * info[Y] + info[Z]
    core = info[C]
    for s in range(4):
        for cr in range(2):
            first = 32 * jnp.bitwise_and(info[X] + 4 - s, 3) + 16 * jnp.bitwise_xor(core, cr)

            def place(y, off, s=s, cr=cr, first=first):
                valid = jnp.where(k < info[OCC + y], info[VIR + y] - first, 0)
                base = off // 8 * 8
                start = off - base
                base = jnp.clip(base - info[PASS] * width + 24, 0, width + 24)
                at = pl.ds(pl.multiple_of(base, 8), 24)
                mine = (row >= start) & (row < start + jnp.minimum(valid, 16))
                here = pl.ds(pl.multiple_of(16 * y, 16), 16)
                for i in range(4):
                    cols = slice(i * 128, (i + 1) * 128)
                    if cr == 1:
                        x = sib[s, i, here, :]
                    elif s == 2:
                        x = jnp.where(core == 0, far0[0, i, here, :], far1[0, i, here, :])
                    else:
                        x = (own, left, None, right)[s][core, i, here, :]
                    x = jnp.pad(x, ((0, 8), (0, 0)))
                    acc[at, cols] = jnp.where(mine, pltpu.roll(x, start, 0), acc[at, cols])
                return off + info[VIR + y]

            lax.fori_loop(0, 8, place, first)

    o_ref[...] = acc[24 : 24 + width, :]


def pack_a(info, parts, after, width):
    full = [pl.BlockSpec(p.shape, lambda i, info: (0, 0, 0, 0)) for p in parts]
    return pl.pallas_call(
        pack_a_kernel,
        grid_spec=pltpu.PrefetchScalarGridSpec(
            num_scalar_prefetch=1,
            grid=(1,),
            in_specs=full + [pl.BlockSpec(memory_space=pl.ANY)],
            out_specs=pl.BlockSpec((width, 512), lambda i, info: (0, 0)),
            scratch_shapes=[pltpu.VMEM((width + 48, 512), F32)],
        ),
        out_shape=jax.ShapeDtypeStruct((width, 512), F32),
        **params(16, name="pack_amplitudes"),
    )(info, *parts, after)


def permute(value, axes, pairs, name):
    with jax.named_scope(name):
        return lax.ppermute(value, axes, pairs)


def shift_y(value, by, name):
    return permute(value, "y", [(p, (p + by) % NY) for p in range(NY)], name)


def shift_x(value, by, name):
    return permute(value, "x", [(p, (p + by) % NX) for p in range(NX)], name)


def swap_core(value, name):
    return permute(value, "c", [(0, 1), (1, 0)], name)


def to_k_owner(value, u, name):
    pairs = []
    for c in range(NC):
        for z in range(NZ):
            pairs.append((c * NZ + z, (z // 2) * NZ + 2 * c + ((z % 2) ^ u)))
    return permute(value, ("c", "z"), pairs, name)


def to_home(value, w, name):
    pairs = []
    for c in range(NC):
        for z in range(NZ):
            pairs.append((c * NZ + z, ((z // 2) ^ w) * NZ + 2 * c + ((z % 2) ^ 1)))
    return permute(value, ("c", "z"), pairs, name)


def to_relay(value0, value1, name):
    first, second = [], []
    for c in range(NC):
        for z in range(NZ):
            at, other = c * NZ + z, 1 if z % 2 == 0 else -1
            if z // 2 == c:
                second.append((at, (1 - c) * NZ + z))
            else:
                first.append((at, c * NZ + (z + other) % NZ))
                second.append((at, c * NZ + (z - other) % NZ))
    return permute(value0, ("c", "z"), first, name), permute(value1, ("c", "z"), second, name)


def products_kernel(info, *refs, plan, first, ws, flat, phase, relayed):
    blocks = 3 if phase == 1 else 4
    refs = refs[1:]
    count = sum(len(g[1]) for g in plan)
    pieces, a_refs, refs = refs[:count], (refs[count : count + blocks], refs[count + blocks : count + 2 * blocks]), refs[count + 2 * blocks :]
    if not first:
        before, refs = refs[0], refs[1:]
    if relayed:
        relay0, relay1, refs = refs[0], refs[1], refs[2:]
    outs, (b_f32, b_both, a_buf, acc, b_sem, a_sem) = refs[:-6], refs[-6:]
    steps = len(plan)
    n = pl.program_id(0)
    w = n // steps
    t = n - w * steps
    rows_all = b_f32.shape[1]

    def away_y(t):
        dx = plan[0][0]
        for at, (other, _) in enumerate(plan[1:]):
            dx = jnp.where(t == at + 1, other, dx)
        return dx, jnp.bitwise_and(info[X] + dx + 4 - info[Y], 3)

    def active(n):
        dx, d = away_y(n - n // steps * steps)
        if phase == 1:
            return d != 2
        if phase == 2:
            return (dx == 2) | (d == 2)
        return n >= 0

    def fetch_a(n, slot):
        w = n // steps
        _, d = away_y(n - w * steps)
        sibling = jnp.bitwise_xor(jnp.bitwise_xor(info[Z] // 2, w + ws[0]), info[C])
        for m, blocks in enumerate(a_refs):
            for way, ref in zip((0, 3, 1, 2), blocks):

                @pl.when((sibling == m) & (d == way))
                def _(ref=ref):
                    for part in range(4):
                        rows = pl.ds(part * (a_buf.shape[1] // 4), a_buf.shape[1] // 4)
                        pltpu.make_async_copy(ref.at[rows], a_buf.at[slot, rows], a_sem.at[slot]).start()

    def b_copies(t):
        at = sum(len(g[1]) for g in plan[:t])
        return [
            pltpu.make_async_copy(pieces[at + p].at[pl.ds(start, rows)], b_f32.at[t, pl.ds(row, rows)], b_sem.at[at + p])
            for p, (row, start, rows) in enumerate(plan[t][1])
        ]

    @pl.when(n == 0)
    def _():
        pl.when(active(0))(lambda: fetch_a(0, 0))
        for t in range(steps):

            @pl.when(active(t))
            def _(t=t):
                for copy in b_copies(t):
                    copy.start()

    @pl.when((n + 1 < len(ws) * steps) & active(n + 1))
    def _():
        fetch_a(n + 1, (n + 1) % 2)

    for at in range(steps):

        @pl.when((n == at) & active(at))
        def _(at=at):
            for copy in b_copies(at):
                copy.wait()
            hi, lo = split(b_f32[at])
            b_both[at, :rows_all, :] = hi
            b_both[at, rows_all:, :] = lo

    @pl.when(t == 0)
    def _():
        acc[...] = jnp.zeros_like(acc) if first else before[...].reshape(acc.shape)

    if relayed:

        @pl.when(n == 0)
        def _():
            acc[...] += jnp.where(info[C] != info[Z] // 2, relay0[...], relay1[...])

    @pl.when(active(n))
    def _():
        slot = n % 2
        pltpu.make_async_copy(a_refs[0][0], a_buf.at[slot], a_sem.at[slot]).wait()

        a_hi, a_lo = split(a_buf[slot])
        new = jnp.dot(b_both[t], a_hi, preferred_element_type=F32)
        acc[...] += new[:rows_all] + new[rows_all:] + jnp.dot(b_both[t, :rows_all, :], a_lo, preferred_element_type=F32)

    for at in range(len(ws)):

        @pl.when(n == (at + 1) * steps - 1)
        def _(at=at):
            if flat:
                outs[at][...] = acc[...]
            else:
                outs[0][0] = acc[...]


def products(info, after, groups, mine, sibling, before=None, ws=(0, 1), flat=True, phase=0, relay=()):
    width, cols = mine[0].shape
    plan, pieces = [], []
    for dx, group in groups:
        row, spans = 0, []
        for piece, start, length in group:
            spans.append((row, start, length))
            row += length
            pieces.append(piece)
        plan.append((dx, tuple(spans)))
    rows, steps = row, len(plan)
    anywhere = pl.BlockSpec(memory_space=pl.ANY)
    both = pl.BlockSpec((1, rows, cols), lambda n, info: (n // steps + ws[0], 0, 0))
    single = pl.BlockSpec((rows, cols), lambda n, info: (0, 0))
    args = [after, *pieces, *mine, *sibling]
    in_specs = [anywhere] * len(args)
    if before is not None:
        args.append(before)
        in_specs.append(both)
    args += relay
    in_specs += [single] * len(relay)
    return pl.pallas_call(
        functools.partial(products_kernel, plan=tuple(plan), first=before is None, ws=ws, flat=flat, phase=phase, relayed=bool(relay)),
        grid_spec=pltpu.PrefetchScalarGridSpec(
            num_scalar_prefetch=1,
            grid=(len(ws) * steps,),
            in_specs=in_specs,
            out_specs=[single] * len(ws) if flat else both,
            scratch_shapes=[
                pltpu.VMEM((steps, rows, width), F32),
                pltpu.VMEM((steps, 2 * rows, width), BF16),
                pltpu.VMEM((2, width, cols), F32),
                pltpu.VMEM((rows, cols), F32),
                pltpu.SemaphoreType.DMA((len(pieces),)),
                pltpu.SemaphoreType.DMA((2,)),
            ],
        ),
        out_shape=[jax.ShapeDtypeStruct((rows, cols), F32)] * len(ws)
        if flat
        else jax.ShapeDtypeStruct((2, rows, cols), F32),
        **params(30, name="products"),
    )(info, *args)


def finish_kernel(info, stayed, came, m2, m3, res, o_ref):
    total = jnp.where(info[C] != info[Z] // 2, came[...], stayed[...]) + (m2[...] + m3[...])
    lane = lax.broadcasted_iota(jnp.int32, (48, 128), 1)
    place = jnp.bitwise_and(lax.broadcasted_iota(jnp.int32, (48, 128), 0), 7)
    keep_a = lane < info[VIR + 2 * info[X] + info[C]]
    for g in range(8):
        rows = slice(48 * g, 48 * (g + 1))
        keep = keep_a & (place < info[VIR + g] - 8 * (4 * info[Y] + info[Z]))
        o_ref[0, rows, :] = res[0, rows, :] + jnp.where(keep, total[rows], 0.0)


def finish(info, messages, residual):
    rows = residual.shape[1]
    part = pl.BlockSpec((rows, 128), lambda i, info: (0, i))
    whole = pl.BlockSpec((1, rows, 128), lambda i, info: (i, 0, 0))
    return pl.pallas_call(
        finish_kernel,
        grid_spec=pltpu.PrefetchScalarGridSpec(
            num_scalar_prefetch=1, grid=(4,), in_specs=[part] * 4 + [whole], out_specs=whole
        ),
        out_shape=jax.ShapeDtypeStruct(residual.shape, F32),
        **params(10, name="finish"),
    )(info, *messages, residual)


def tie(value, *deps, cost=COST):
    anywhere = pl.BlockSpec(memory_space=pl.ANY)
    return pl.pallas_call(
        stage_kernel,
        in_specs=[anywhere] * (1 + len(deps)),
        out_specs=anywhere,
        out_shape=jax.ShapeDtypeStruct(value.shape, value.dtype),
        input_output_aliases={0: 0},
        cost_estimate=cost,
        name="tie",
    )(value, *deps)


def stage_kernel(*refs):
    pass


def stage(*values):
    anywhere = pl.BlockSpec(memory_space=pl.ANY)
    return pl.pallas_call(
        stage_kernel,
        in_specs=[anywhere] * len(values),
        out_specs=[anywhere] * len(values),
        out_shape=[jax.ShapeDtypeStruct(v.shape, v.dtype) for v in values],
        input_output_aliases={n: n for n in range(len(values))},
        cost_estimate=COST,
        name="stage",
    )(*values)


def body(amplitudes, coupling, incoming_residual, occupied_count, virtual_count):
    kept = jnp.sum(virtual_count)
    narrow, wide = WIDTHS
    info = scalars(occupied_count, virtual_count)

    amps = amplitudes.reshape(4, 2, 4, 128, 128)
    coupling_rows = coupling.reshape(-1, 128)

    def one(width, n, residual):
        numbered = jnp.concatenate([info, jnp.full((1,), n, jnp.int32)])
        return packed_body(amps, coupling_rows, residual, numbered, width=width)

    return lax.cond(
        kept <= narrow,
        lambda residual: one(narrow, 0, residual),
        lambda residual: lax.fori_loop(
            0, (kept + wide - 1) // wide, functools.partial(one, wide), jnp.where(kept > narrow, residual, 0.0)
        ),
        incoming_residual,
    )


def packed_body(amps, coupling_rows, incoming_residual, info, *, width):
    xi, ci = lax.axis_index("x"), lax.axis_index("c")

    def at(by):
        return lax.dynamic_index_in_dim(amps, (xi + by) % 4, 0, keepdims=False)

    own, two_away = at(0), at(2)
    to_right = jnp.concatenate([at(1), two_away[:1]])
    to_left = jnp.concatenate([at(3), two_away[1:]])
    left, right = shift_x(to_right, 1, "amps_left"), shift_x(to_left, -1, "amps_right")
    packed = pack_b(info, coupling_rows, to_right, width)
    via_left, via_right = left[2:], right[2:]
    via_left, via_right, p0, p1 = stage(via_left, via_right, *packed)
    far0, far1 = shift_x(via_left, 1, "amps_far0"), shift_x(via_right, -1, "amps_far1")
    b0, b1 = (to_k_owner(p, u, "coupling_to_k") for u, p in zip(ORDER, (p0, p1)))

    def other(value):
        return lax.dynamic_index_in_dim(value, 1 - ci, 0, keepdims=False)

    sib = swap_core(
        jnp.stack([other(own), other(left), jnp.where(ci == 0, far1[0], far0[0]), other(right)]), "amps_sibling"
    )
    packed_a = pack_a(info, (own, left, right, far0, far1, sib), p0, width)

    rows = b0.shape[0]
    mid = rows // 2
    b0, _, _ = stage(b0, far0, far1)
    left0, right0 = shift_x(b0, 1, "b0_left"), shift_x(b0, -1, "b0_right")
    left1 = shift_x(jnp.concatenate([b1, left0[:mid]]), 1, "b1_left")
    right1 = shift_x(jnp.concatenate([b1, right0[mid:]]), -1, "b1_right")
    top = tie(left1[:mid], right1, cost=LONG)
    left2 = shift_x(top, 1, "b2_left")
    right2 = shift_x(right1[mid:rows], -1, "b2_right")

    half = width // 2
    a_left, a_right = shift_y(packed_a, 1, "a_left"), shift_y(packed_a, -1, "a_right")
    a_top = tie(a_left[:half], left0, right0)
    a_far = jnp.concatenate([shift_y(a_top, 1, "a_top"), shift_y(a_right[half:], -1, "a_low")])
    mine = (packed_a, a_left, a_right, a_far)
    sibling = tuple(swap_core(m, "a_sibling") for m in mine)

    near0 = [(0, [(b0, 0, rows)]), (-1, [(left0, 0, rows)]), (1, [(right0, 0, rows)])]
    far0 = [(2, [(left1, rows, mid), (right1, rows, mid)])]
    near1 = [(0, [(b1, 0, rows)]), (-1, [(left1, 0, rows)]), (1, [(right1, 0, rows)])]
    far1 = [(2, [(left2, 0, mid), (right2, 0, mid)])]
    sent0 = products(info, top, near0 + far0, mine, sibling)
    acc1 = products(info, sent0[0], near1, mine, sibling, flat=False)
    relay = to_relay(*sent0, "home0")
    sent1 = products(info, acc1, far1, mine, sibling, acc1, relay=relay)
    total = [sent0[0], relay[1], *(to_home(sent1[w], w, "home1") for w in range(2))]
    return finish(info, total, incoming_residual.reshape(4, 384, 128)).reshape(incoming_residual.shape)


def solution(mesh):
    fine = Mesh(mesh.devices.reshape(NX, NC, NY, NZ), ("x", "c", "y", "z"))
    return jax.shard_map(
        body,
        mesh=fine,
        in_specs=(
            P(None, None, None, ("y", "z"), ("x", "c"), None),
            P(None, None, ("y", "z"), None, ("x", "c"), None),
            P(("x", "c"), None, None, None, ("y", "z"), None),
            P(),
            P(),
        ),
        out_specs=P(("x", "c"), None, None, None, ("y", "z"), None),
        check_vma=False,
    )
```

```python
import functools

import jax
import jax.numpy as jnp
from jax import lax
from jax.experimental import pallas as pl
from jax.experimental.pallas import tpu as pltpu
from jax.sharding import Mesh
from jax.sharding import PartitionSpec as P

NX, NC, NY, NZ = 4, 2, 4, 4
F32 = jnp.float32
BF16 = jnp.bfloat16
ORDER = (0, 1)
WIDTHS = (768, 896)
TILE = 256
COST = pl.CostEstimate(flops=1, bytes_accessed=1, transcendentals=0)
LONG = pl.CostEstimate(flops=2 * 10**10, bytes_accessed=7 * 10**7, transcendentals=0)


def split(x):
    hi = x.astype(BF16)
    lo = (x - hi.astype(F32)).astype(BF16)
    return hi, lo


VIR, OCC, X, C, Y, Z, PASS = 0, 8, 16, 17, 18, 19, 20


def scalars(occupied_count, virtual_count):
    place = jnp.stack([lax.axis_index(n) for n in ("x", "c", "y", "z")])
    return jnp.concatenate([virtual_count, occupied_count, place]).astype(jnp.int32)


def params(mib, **more):
    return dict(compiler_params=pltpu.CompilerParams(vmem_limit_bytes=mib * 2**20), cost_estimate=COST, **more)


ROWS_B = 96


def pack_b_kernel(info, b_ref, after, *refs):
    outs, acc = refs[:2], refs[2]
    width = outs[0].shape[1]
    lane = lax.broadcasted_iota(jnp.int32, (ROWS_B, 128), 1)
    for u, o_ref in zip(ORDER, outs):
        e = jnp.bitwise_xor(jnp.bitwise_and(info[Z], 1), u)
        acc[...] = jnp.zeros_like(acc)

        def place(y, off):
            count = info[VIR + y]
            tile = off // 128
            start = off - tile * 128
            tile = jnp.clip(tile - info[PASS] * (width // 128) + 2, 0, width // 128 + 2)
            x = pltpu.roll(b_ref[pl.ds(2 * y + e, ROWS_B, stride=16), :], start, 1)
            here = pl.ds(pl.multiple_of(tile * 128, 128), 128)
            there = pl.ds(pl.multiple_of(tile * 128 + 128, 128), 128)
            acc[:, here] += jnp.where((lane >= start) & (lane < start + count), x, 0.0)
            acc[:, there] += jnp.where(lane < start + count - 128, x, 0.0)
            return off + count

        lax.fori_loop(0, 8, place, 0)
        o_ref[...] = acc[:, 256 : 256 + width]


def pack_b(info, b2, after, width):
    rows = b2.shape[0] // 16
    out = pl.BlockSpec((ROWS_B, width), lambda r, info: (r, 0))
    return pl.pallas_call(
        pack_b_kernel,
        grid_spec=pltpu.PrefetchScalarGridSpec(
            num_scalar_prefetch=1,
            grid=(rows // ROWS_B,),
            in_specs=[
                pl.BlockSpec((ROWS_B * 16, 128), lambda r, info: (r, 0)),
                pl.BlockSpec(memory_space=pl.ANY),
            ],
            out_specs=[out, out],
            scratch_shapes=[pltpu.VMEM((ROWS_B, width + 512), F32)],
        ),
        out_shape=[jax.ShapeDtypeStruct((rows, width), F32)] * 2,
        **params(12, name="pack_coupling"),
    )(info, b2, after)


def pack_a_kernel(info, own, left, right, far0, far1, sib, after, o_ref, acc):
    width = o_ref.shape[0]
    acc[...] = jnp.zeros_like(acc)
    row = lax.broadcasted_iota(jnp.int32, (24, 128), 0)
    k = 4 * info[Y] + info[Z]
    core = info[C]
    for s in range(4):
        for cr in range(2):
            first = 32 * jnp.bitwise_and(info[X] + 4 - s, 3) + 16 * jnp.bitwise_xor(core, cr)

            def place(y, off, s=s, cr=cr, first=first):
                valid = jnp.where(k < info[OCC + y], info[VIR + y] - first, 0)
                base = off // 8 * 8
                start = off - base
                base = jnp.clip(base - info[PASS] * width + 24, 0, width + 24)
                at = pl.ds(pl.multiple_of(base, 8), 24)
                mine = (row >= start) & (row < start + jnp.minimum(valid, 16))
                here = pl.ds(pl.multiple_of(16 * y, 16), 16)
                for i in range(4):
                    cols = slice(i * 128, (i + 1) * 128)
                    if cr == 1:
                        x = sib[s, i, here, :]
                    elif s == 2:
                        x = jnp.where(core == 0, far0[0, i, here, :], far1[0, i, here, :])
                    else:
                        x = (own, left, None, right)[s][core, i, here, :]
                    x = jnp.pad(x, ((0, 8), (0, 0)))
                    acc[at, cols] = jnp.where(mine, pltpu.roll(x, start, 0), acc[at, cols])
                return off + info[VIR + y]

            lax.fori_loop(0, 8, place, first)

    o_ref[...] = acc[24 : 24 + width, :]


def pack_a(info, parts, after, width):
    full = [pl.BlockSpec(p.shape, lambda i, info: (0, 0, 0, 0)) for p in parts]
    return pl.pallas_call(
        pack_a_kernel,
        grid_spec=pltpu.PrefetchScalarGridSpec(
            num_scalar_prefetch=1,
            grid=(1,),
            in_specs=full + [pl.BlockSpec(memory_space=pl.ANY)],
            out_specs=pl.BlockSpec((width, 512), lambda i, info: (0, 0)),
            scratch_shapes=[pltpu.VMEM((width + 48, 512), F32)],
        ),
        out_shape=jax.ShapeDtypeStruct((width, 512), F32),
        **params(16, name="pack_amplitudes"),
    )(info, *parts, after)


def permute(value, axes, pairs, name):
    with jax.named_scope(name):
        return lax.ppermute(value, axes, pairs)


def shift_y(value, by, name):
    return permute(value, "y", [(p, (p + by) % NY) for p in range(NY)], name)


def shift_x(value, by, name):
    return permute(value, "x", [(p, (p + by) % NX) for p in range(NX)], name)


def swap_core(value, name):
    return permute(value, "c", [(0, 1), (1, 0)], name)


def to_k_owner(value, u, name):
    pairs = []
    for c in range(NC):
        for z in range(NZ):
            pairs.append((c * NZ + z, (z // 2) * NZ + 2 * c + ((z % 2) ^ u)))
    return permute(value, ("c", "z"), pairs, name)


def to_home(value, w, name):
    pairs = []
    for c in range(NC):
        for z in range(NZ):
            pairs.append((c * NZ + z, ((z // 2) ^ w) * NZ + 2 * c + ((z % 2) ^ 1)))
    return permute(value, ("c", "z"), pairs, name)


def to_relay(value0, value1, name):
    first, second = [], []
    for c in range(NC):
        for z in range(NZ):
            at, other = c * NZ + z, 1 if z % 2 == 0 else -1
            if z // 2 == c:
                second.append((at, (1 - c) * NZ + z))
            else:
                first.append((at, c * NZ + (z + other) % NZ))
                second.append((at, c * NZ + (z - other) % NZ))
    return permute(value0, ("c", "z"), first, name), permute(value1, ("c", "z"), second, name)


def products_kernel(info, *refs, plan, first, ws, flat, phase, relayed):
    blocks = 3 if phase == 1 else 4
    refs = refs[1:]
    count = sum(len(g[1]) for g in plan)
    pieces, a_refs, refs = refs[:count], (refs[count : count + blocks], refs[count + blocks : count + 2 * blocks]), refs[count + 2 * blocks :]
    if not first:
        before, refs = refs[0], refs[1:]
    if relayed:
        relay0, relay1, refs = refs[0], refs[1], refs[2:]
    outs, (b_f32, b_both, a_buf, acc, b_sem, a_sem) = refs[:-6], refs[-6:]
    steps = len(plan)
    n = pl.program_id(0)
    w = n // steps
    t = n - w * steps
    rows_all = b_f32.shape[1]

    def away_y(t):
        dx = plan[0][0]
        for at, (other, _) in enumerate(plan[1:]):
            dx = jnp.where(t == at + 1, other, dx)
        return dx, jnp.bitwise_and(info[X] + dx + 4 - info[Y], 3)

    def active(n):
        dx, d = away_y(n - n // steps * steps)
        if phase == 1:
            return d != 2
        if phase == 2:
            return (dx == 2) | (d == 2)
        return n >= 0

    def fetch_a(n, slot):
        w = n // steps
        _, d = away_y(n - w * steps)
        sibling = jnp.bitwise_xor(jnp.bitwise_xor(info[Z] // 2, w + ws[0]), info[C])
        for m, blocks in enumerate(a_refs):
            for way, ref in zip((0, 3, 1, 2), blocks):

                @pl.when((sibling == m) & (d == way))
                def _(ref=ref):
                    for part in range(4):
                        rows = pl.ds(part * (a_buf.shape[1] // 4), a_buf.shape[1] // 4)
                        pltpu.make_async_copy(ref.at[rows], a_buf.at[slot, rows], a_sem.at[slot]).start()

    def b_copies(t):
        at = sum(len(g[1]) for g in plan[:t])
        return [
            pltpu.make_async_copy(pieces[at + p].at[pl.ds(start, rows)], b_f32.at[t, pl.ds(row, rows)], b_sem.at[at + p])
            for p, (row, start, rows) in enumerate(plan[t][1])
        ]

    @pl.when(n == 0)
    def _():
        pl.when(active(0))(lambda: fetch_a(0, 0))
        for t in range(steps):

            @pl.when(active(t))
            def _(t=t):
                for copy in b_copies(t):
                    copy.start()

    @pl.when((n + 1 < len(ws) * steps) & active(n + 1))
    def _():
        fetch_a(n + 1, (n + 1) % 2)

    for at in range(steps):

        @pl.when((n == at) & active(at))
        def _(at=at):
            for copy in b_copies(at):
                copy.wait()
            hi, lo = split(b_f32[at])
            b_both[at, :rows_all, :] = hi
            b_both[at, rows_all:, :] = lo

    @pl.when(t == 0)
    def _():
        acc[...] = jnp.zeros_like(acc) if first else before[...].reshape(acc.shape)

    if relayed:

        @pl.when(n == 0)
        def _():
            acc[...] += jnp.where(info[C] != info[Z] // 2, relay0[...], relay1[...])

    @pl.when(active(n))
    def _():
        slot = n % 2
        pltpu.make_async_copy(a_refs[0][0], a_buf.at[slot], a_sem.at[slot]).wait()

        a_hi, a_lo = split(a_buf[slot])
        new = jnp.dot(b_both[t], a_hi, preferred_element_type=F32)
        acc[...] += new[:rows_all] + new[rows_all:] + jnp.dot(b_both[t, :rows_all, :], a_lo, preferred_element_type=F32)

    for at in range(len(ws)):

        @pl.when(n == (at + 1) * steps - 1)
        def _(at=at):
            if flat:
                outs[at][...] = acc[...]
            else:
                outs[0][0] = acc[...]


def products(info, after, groups, mine, sibling, before=None, ws=(0, 1), flat=True, phase=0, relay=()):
    width, cols = mine[0].shape
    plan, pieces = [], []
    for dx, group in groups:
        row, spans = 0, []
        for piece, start, length in group:
            spans.append((row, start, length))
            row += length
            pieces.append(piece)
        plan.append((dx, tuple(spans)))
    rows, steps = row, len(plan)
    anywhere = pl.BlockSpec(memory_space=pl.ANY)
    both = pl.BlockSpec((1, rows, cols), lambda n, info: (n // steps + ws[0], 0, 0))
    single = pl.BlockSpec((rows, cols), lambda n, info: (0, 0))
    args = [after, *pieces, *mine, *sibling]
    in_specs = [anywhere] * len(args)
    if before is not None:
        args.append(before)
        in_specs.append(both)
    args += relay
    in_specs += [single] * len(relay)
    return pl.pallas_call(
        functools.partial(products_kernel, plan=tuple(plan), first=before is None, ws=ws, flat=flat, phase=phase, relayed=bool(relay)),
        grid_spec=pltpu.PrefetchScalarGridSpec(
            num_scalar_prefetch=1,
            grid=(len(ws) * steps,),
            in_specs=in_specs,
            out_specs=[single] * len(ws) if flat else both,
            scratch_shapes=[
                pltpu.VMEM((steps, rows, width), F32),
                pltpu.VMEM((steps, 2 * rows, width), BF16),
                pltpu.VMEM((2, width, cols), F32),
                pltpu.VMEM((rows, cols), F32),
                pltpu.SemaphoreType.DMA((len(pieces),)),
                pltpu.SemaphoreType.DMA((2,)),
            ],
        ),
        out_shape=[jax.ShapeDtypeStruct((rows, cols), F32)] * len(ws)
        if flat
        else jax.ShapeDtypeStruct((2, rows, cols), F32),
        **params(30, name="products"),
    )(info, *args)


def finish_kernel(info, stayed, came, m2, m3, res, o_ref):
    total = jnp.where(info[C] != info[Z] // 2, came[...], stayed[...]) + (m2[...] + m3[...])
    lane = lax.broadcasted_iota(jnp.int32, (48, 128), 1)
    place = jnp.bitwise_and(lax.broadcasted_iota(jnp.int32, (48, 128), 0), 7)
    keep_a = lane < info[VIR + 2 * info[X] + info[C]]
    for g in range(8):
        rows = slice(48 * g, 48 * (g + 1))
        keep = keep_a & (place < info[VIR + g] - 8 * (4 * info[Y] + info[Z]))
        o_ref[0, rows, :] = res[0, rows, :] + jnp.where(keep, total[rows], 0.0)


def finish(info, messages, residual):
    rows = residual.shape[1]
    part = pl.BlockSpec((rows, 128), lambda i, info: (0, i))
    whole = pl.BlockSpec((1, rows, 128), lambda i, info: (i, 0, 0))
    return pl.pallas_call(
        finish_kernel,
        grid_spec=pltpu.PrefetchScalarGridSpec(
            num_scalar_prefetch=1, grid=(4,), in_specs=[part] * 4 + [whole], out_specs=whole
        ),
        out_shape=jax.ShapeDtypeStruct(residual.shape, F32),
        **params(10, name="finish"),
    )(info, *messages, residual)


def tie(value, *deps, cost=COST):
    anywhere = pl.BlockSpec(memory_space=pl.ANY)
    return pl.pallas_call(
        stage_kernel,
        in_specs=[anywhere] * (1 + len(deps)),
        out_specs=anywhere,
        out_shape=jax.ShapeDtypeStruct(value.shape, value.dtype),
        input_output_aliases={0: 0},
        cost_estimate=cost,
        name="tie",
    )(value, *deps)


def stage_kernel(*refs):
    pass


def stage(*values):
    anywhere = pl.BlockSpec(memory_space=pl.ANY)
    return pl.pallas_call(
        stage_kernel,
        in_specs=[anywhere] * len(values),
        out_specs=[anywhere] * len(values),
        out_shape=[jax.ShapeDtypeStruct(v.shape, v.dtype) for v in values],
        input_output_aliases={n: n for n in range(len(values))},
        cost_estimate=COST,
        name="stage",
    )(*values)


def body(amplitudes, coupling, incoming_residual, occupied_count, virtual_count):
    kept = jnp.sum(virtual_count)
    narrow, wide = WIDTHS
    info = scalars(occupied_count, virtual_count)

    amps = amplitudes.reshape(4, 2, 4, 128, 128)
    coupling_rows = coupling.reshape(-1, 128)

    def one(width, n, residual):
        numbered = jnp.concatenate([info, jnp.full((1,), n, jnp.int32)])
        return packed_body(amps, coupling_rows, residual, numbered, width=width)

    return lax.cond(
        kept <= narrow,
        lambda residual: one(narrow, 0, residual),
        lambda residual: lax.fori_loop(
            0, (kept + wide - 1) // wide, functools.partial(one, wide), jnp.where(kept > narrow, residual, 0.0)
        ),
        incoming_residual,
    )


def packed_body(amps, coupling_rows, incoming_residual, info, *, width):
    xi, ci = lax.axis_index("x"), lax.axis_index("c")

    def at(by):
        return lax.dynamic_index_in_dim(amps, (xi + by) % 4, 0, keepdims=False)

    own, two_away = at(0), at(2)
    to_right = jnp.concatenate([at(1), two_away[:1]])
    to_left = jnp.concatenate([at(3), two_away[1:]])
    left, right = shift_x(to_right, 1, "amps_left"), shift_x(to_left, -1, "amps_right")
    packed = pack_b(info, coupling_rows, to_right, width)
    via_left, via_right = left[2:], right[2:]
    via_left, via_right, p0, p1 = stage(via_left, via_right, *packed)
    far0, far1 = shift_x(via_left, 1, "amps_far0"), shift_x(via_right, -1, "amps_far1")
    b0, b1 = (to_k_owner(p, u, "coupling_to_k") for u, p in zip(ORDER, (p0, p1)))

    def other(value):
        return lax.dynamic_index_in_dim(value, 1 - ci, 0, keepdims=False)

    sib = swap_core(
        jnp.stack([other(own), other(left), jnp.where(ci == 0, far1[0], far0[0]), other(right)]), "amps_sibling"
    )
    packed_a = pack_a(info, (own, left, right, far0, far1, sib), p0, width)

    rows = b0.shape[0]
    mid = rows // 2
    b0, _, _ = stage(b0, far0, far1)
    left0, right0 = shift_x(b0, 1, "b0_left"), shift_x(b0, -1, "b0_right")
    left1 = shift_x(jnp.concatenate([b1, left0[:mid]]), 1, "b1_left")
    right1 = shift_x(jnp.concatenate([b1, right0[mid:]]), -1, "b1_right")
    top = tie(left1[:mid], right1, cost=LONG)
    left2 = shift_x(top, 1, "b2_left")
    right2 = shift_x(right1[mid:rows], -1, "b2_right")

    half = width // 2
    a_left, a_right = shift_y(packed_a, 1, "a_left"), shift_y(packed_a, -1, "a_right")
    a_top = tie(a_left[:half], left0, right0)
    a_far = jnp.concatenate([shift_y(a_top, 1, "a_top"), shift_y(a_right[half:], -1, "a_low")])
    mine = (packed_a, a_left, a_right, a_far)
    sibling = tuple(swap_core(m, "a_sibling") for m in mine)

    near0 = [(0, [(b0, 0, rows)]), (-1, [(left0, 0, rows)]), (1, [(right0, 0, rows)])]
    far0 = [(2, [(left1, rows, mid), (right1, rows, mid)])]
    near1 = [(0, [(b1, 0, rows)]), (-1, [(left1, 0, rows)]), (1, [(right1, 0, rows)])]
    far1 = [(2, [(left2, 0, mid), (right2, 0, mid)])]
    sent0 = products(info, top, near0 + far0, mine, sibling)
    acc1 = products(info, sent0[0], near1, mine, sibling, flat=False)
    relay = to_relay(*sent0, "home0")
    sent1 = products(info, acc1, far1, mine, sibling, acc1, (0,), relay=relay)
    sent1 += products(info, acc1, far1, mine, sibling, acc1, (1,))
    total = [sent0[0], relay[1], *(to_home(sent1[w], w, "home1") for w in range(2))]
    return finish(info, total, incoming_residual.reshape(4, 384, 128)).reshape(incoming_residual.shape)


def solution(mesh):
    fine = Mesh(mesh.devices.reshape(NX, NC, NY, NZ), ("x", "c", "y", "z"))
    return jax.shard_map(
        body,
        mesh=fine,
        in_specs=(
            P(None, None, None, ("y", "z"), ("x", "c"), None),
            P(None, None, ("y", "z"), None, ("x", "c"), None),
            P(("x", "c"), None, None, None, ("y", "z"), None),
            P(),
            P(),
        ),
        out_specs=P(("x", "c"), None, None, None, ("y", "z"), None),
        check_vma=False,
    )
```
